128 devices in a mesh: dp: 8 (over x_hi, z), fsdp: 16 (over y, x_lo, core).
Axes of the slice: x: 4 (x_hi: 2, x_lo: 2; x = x_hi * 2 + x_lo), y: 4, z: 4, core: 2. Of those that a mesh axis runs over, the one named last changes fastest.
Arguments:
- queries: bfloat16 [36864, 3072], P(('dp', 'fsdp')), may hold values from -8 to 8
- key_vectors: bfloat16 [36864, 3072], P(('dp', 'fsdp')), may hold values from -8 to 8
- value_vectors: bfloat16 [36864, 3072], P(('dp', 'fsdp')), may hold values from -6 to 6
- image_lengths: int32 [128, 6], replicated, may hold values from 16 to 208, as said below
- image_dest: int32 [128, 6], replicated, may hold values from 0 to 7, as said below
- image_offset: int32 [128, 6], replicated, may hold values from 0 to 272, as said below
- out_weight: bfloat16 [3072, 3072], P('fsdp'), may hold values from -0.109375 to 0.109375
- out_grad: bfloat16 [36864, 3072], P(('dp', 'fsdp')), may hold values from -24 to 24
Outputs:
- projected: bfloat16 [36864, 3072], P(('dp', 'fsdp'))
- query_grad: bfloat16 [36864, 3072], P(('dp', 'fsdp'))
- key_grad: bfloat16 [36864, 3072], P(('dp', 'fsdp'))
- value_grad: bfloat16 [36864, 3072], P(('dp', 'fsdp'))
- weight_grad: bfloat16 [3072, 3072], P('fsdp', 'dp')
The draws below stay inside these ranges and needn't reach their ends.
Inputs may be any that keep to these rules, and one draw needn't show every extreme that they name: `image_lengths`: every length is a multiple of 16; the lengths of one device sum to 288; every device holds at least three images of exactly 16 patches; in each group of devices that share an fsdp index, at least one device holds an image of exactly 208 patches. `image_dest`: A device's image keeps its dp index or moves to another device with the same fsdp index. Each device sends exactly three images, each of 16 patches, to three different devices, and receives three such images. `image_offset`: offsets are multiples of 16; the images that land on one device, kept and received, cover its 288 rows exactly, without intersection.
All inputs are finite; a program needn't handle non-finite values.
Results may differ from the reference program's by a relative error of at most 0.025.
Values may be sent and summed in bfloat16 or wider, within the bound.
A program may use at most 192 MiB of HBM per device.

```python
import jax
import jax.numpy as jnp
from jax import lax

D = 3072
HD = 128
HH = 3072
ROWS = 288
SLOT = 16
IMG_DEV = 6
MAXLEN = 208
TOKENS = 36864
N_DP = 8
N_FSDP = 16


def plan_group(key):
    unit_count = ROWS // SLOT
    most_units = MAXLEN // SLOT
    subkeys = jax.random.split(key, 8)
    dev_ids = jnp.arange(N_DP, dtype=jnp.int32)
    big_dev = jax.random.randint(subkeys[0], (), 0, N_DP)
    big_len = jax.random.randint(subkeys[1], (N_DP,), 2, most_units + 1)
    big_len = jnp.where(dev_ids == big_dev, most_units, big_len)
    rest_len = unit_count - 3 - big_len
    first_len = jax.random.randint(subkeys[2], (N_DP,), 0, 1 << 20) % (rest_len - 1) + 1
    second_len = rest_len - first_len
    ones_three = jnp.ones((N_DP, 3), jnp.int32)
    canon_units = jnp.concatenate([ones_three, jnp.stack([big_len, first_len, second_len], axis=1)], axis=1)
    cycle_order = jax.random.permutation(subkeys[3], N_DP).astype(jnp.int32)
    position = jnp.zeros((N_DP,), jnp.int32).at[cycle_order].set(dev_ids)
    shifts = (jax.random.permutation(subkeys[4], N_DP - 1)[:3] + 1).astype(jnp.int32)
    send_to = cycle_order[(position[:, None] + shifts[None, :]) % N_DP]
    item_order = jax.vmap(lambda subkey: jax.random.permutation(subkey, IMG_DEV))(jax.random.split(subkeys[5], N_DP)).astype(jnp.int32)
    forced_order = jnp.concatenate([(jax.random.permutation(subkeys[7], IMG_DEV - 1) + 1).astype(jnp.int32), jnp.zeros((1,), jnp.int32)])
    item_order = jnp.where((dev_ids == big_dev)[:, None], forced_order[None, :], item_order).astype(jnp.int32)
    ordered_units = jnp.take_along_axis(canon_units, item_order, axis=1)
    ordered_start = (jnp.cumsum(ordered_units, axis=1) - ordered_units).astype(jnp.int32)
    item_offset = jnp.zeros((N_DP, IMG_DEV), jnp.int32).at[dev_ids[:, None], item_order].set(ordered_start)
    send_offset = item_offset[send_to, jnp.arange(3, dtype=jnp.int32)[None, :]]
    canon_dest = jnp.concatenate([send_to, jnp.broadcast_to(dev_ids[:, None], (N_DP, 3))], axis=1)
    canon_offset = jnp.concatenate([send_offset, item_offset[:, 3:]], axis=1)
    shuffle = jax.vmap(lambda subkey: jax.random.permutation(subkey, IMG_DEV))(jax.random.split(subkeys[6], N_DP)).astype(jnp.int32)
    lengths_out = jnp.take_along_axis(canon_units, shuffle, axis=1) * SLOT
    dest_out = jnp.take_along_axis(canon_dest, shuffle, axis=1)
    offset_out = jnp.take_along_axis(canon_offset, shuffle, axis=1) * SLOT
    return (lengths_out.astype(jnp.int32), dest_out.astype(jnp.int32), offset_out.astype(jnp.int32))


def plan(key):
    lengths_out, dest_out, offset_out = jax.vmap(plan_group)(jax.random.split(key, N_FSDP))

    def arrange(table):
        return jnp.transpose(table, (1, 0, 2)).reshape(N_DP * N_FSDP, IMG_DEV)
    return (arrange(lengths_out), arrange(dest_out), arrange(offset_out))


def draw_queries(key, part):
    key = jax.random.fold_in(key, 3)
    return jnp.clip(2.0 * jax.random.normal(key, (TOKENS, HH), jnp.float32), -8.0, 8.0).astype(jnp.bfloat16)


def draw_key_vectors(key, part):
    key = jax.random.fold_in(key, 4)
    return jnp.clip(2.0 * jax.random.normal(key, (TOKENS, HH), jnp.float32), -8.0, 8.0).astype(jnp.bfloat16)


def draw_image_lengths(key, part):
    shared = plan(key)
    return shared[0]


def draw_image_dest(key, part):
    shared = plan(key)
    return shared[1]


def draw_image_offset(key, part):
    shared = plan(key)
    return shared[2]


def strengthened(entries, key, source, target, blocks, factor):
    owner, partner = [(jnp.arange(entries.shape[axis_at]) // (entries.shape[axis_at] // blocks)).reshape([-1 if axis == axis_at else 1 for axis in range(entries.ndim)]) for axis_at in (source, target)]
    chosen = jax.random.permutation(key, blocks)[partner]
    strong = (owner == chosen) | (owner == (partner + blocks // 2) % blocks)
    return jnp.where(strong, factor * entries, entries)


def shard_levels(stream_key, shape, shards, smallest, largest):
    def one(axis_at, blocks):
        heights = jax.random.uniform(jax.random.fold_in(jax.random.fold_in(stream_key, 6), axis_at), (blocks,), jnp.float32, smallest / len(shards), largest / len(shards))
        return jnp.repeat(jnp.exp(heights), shape[axis_at] // blocks).reshape((-1,) + (1,) * (len(shape) - axis_at - 1))

    level = one(*shards[0])
    for cut in shards[1:]:
        level = level * one(*cut)
    return level


def gaussian(key, dims, deviation, limit, pieces=(), kind=jnp.bfloat16):
    array = deviation * jax.random.normal(key, dims, jnp.float32)
    if pieces:
        array = array * shard_levels(key, dims, pieces, -0.22, 0.18)
    return jnp.clip(array, -limit, limit).astype(kind)


def heavy_noise(stream_key, shape, scale, limit, cuts, heavy, kind=jnp.bfloat16):
    result = scale * jax.random.normal(stream_key, shape, jnp.float32)
    if cuts:
        result = result * shard_levels(stream_key, shape, cuts, -0.22, 0.18)
    return jnp.clip(strengthened(result, jax.random.fold_in(stream_key, 3), *heavy), -limit, limit).astype(kind)


def setup_inputs(seed: int = 0) -> dict:
    arg_keys = jax.random.split(jax.random.key(seed), 9)
    queries = draw_queries(jax.random.fold_in(arg_keys[8], 71), 0)
    key_vectors = draw_key_vectors(jax.random.fold_in(arg_keys[8], 71), 0)
    value_vectors = gaussian(arg_keys[2], (TOKENS, HH), 1.0, 6.0, ((0, 128),))
    image_lengths = draw_image_lengths(jax.random.fold_in(arg_keys[8], 71), 0)
    image_dest = draw_image_dest(jax.random.fold_in(arg_keys[8], 71), 0)
    image_offset = draw_image_offset(jax.random.fold_in(arg_keys[8], 71), 0)
    out_weight = gaussian(arg_keys[6], (HH, D), HH ** -0.5, 0.109375, ((0, 16),))
    out_grad = heavy_noise(arg_keys[7], (TOKENS, D), 1.0, 24.0, ((0, 128),), (0, 1, 128, 5.5))
    return dict(queries=queries, key_vectors=key_vectors, value_vectors=value_vectors, image_lengths=image_lengths, image_dest=image_dest, image_offset=image_offset, out_weight=out_weight, out_grad=out_grad)


def attention(query_rows, key_rows, value_rows, same_image):
    row_count = query_rows.shape[0]
    head_count = query_rows.shape[1] // HD
    query_heads = query_rows.reshape(row_count, head_count, HD).astype(jnp.float32)
    key_heads = key_rows.reshape(row_count, head_count, HD).astype(jnp.float32)
    value_heads = value_rows.reshape(row_count, head_count, HD).astype(jnp.float32)
    scores = jnp.einsum('ahd,bhd->hab', query_heads, key_heads) * HD ** (-0.5)
    scores = jnp.where(same_image[None, :, :], scores, -1e+30)
    row_max = lax.stop_gradient(lax.optimization_barrier(jnp.max(scores, axis=2, keepdims=True)))
    powers = jnp.exp(scores - row_max)
    weights = (powers / lax.optimization_barrier(jnp.sum(powers, axis=2, keepdims=True))).astype(jnp.bfloat16)
    mixed = jnp.einsum('hab,bhd->ahd', weights.astype(jnp.float32), value_heads)
    return mixed.reshape(row_count, head_count * HD).astype(jnp.bfloat16)

def layout(image_lengths, image_dest, image_offset):
    dev_count = image_lengths.shape[0]
    img_count = image_lengths.shape[1]
    starts = (jnp.cumsum(image_lengths, axis=1) - image_lengths).astype(jnp.int32)
    device = jnp.arange(dev_count, dtype=jnp.int32)[:, None]
    target = (image_dest * N_FSDP + device % N_FSDP).astype(jnp.int32)
    row_ids = jnp.arange(ROWS, dtype=jnp.int32)
    inside = (row_ids[None, None, :] >= starts[:, :, None]) & (row_ids[None, None, :] < (starts + image_lengths)[:, :, None])
    moved_base = (target * ROWS + image_offset - starts).astype(jnp.int32)
    row_place = lax.optimization_barrier(jnp.sum(jnp.where(inside, moved_base[:, :, None] + row_ids[None, None, :], 0), axis=1)).astype(jnp.int32)
    image_ids = (device * img_count + jnp.arange(img_count, dtype=jnp.int32)[None, :]).astype(jnp.int32)
    image_id = lax.optimization_barrier(jnp.sum(jnp.where(inside, image_ids[:, :, None], 0), axis=1)).astype(jnp.int32)
    return (row_place.reshape(-1), image_id.reshape(-1))

def reference(queries, key_vectors, value_vectors, image_lengths, image_dest, image_offset, out_weight, out_grad):
    row_place, image_id = layout(image_lengths, image_dest, image_offset)
    row_total = row_place.shape[0]
    dev_count = image_lengths.shape[0]
    col_count = queries.shape[1]
    inverse_place = jnp.zeros((row_total,), jnp.int32).at[row_place].set(jnp.arange(row_total, dtype=jnp.int32))

    def blocks(matrix):
        return matrix[inverse_place].reshape(dev_count, ROWS, matrix.shape[1])
    moved_q = blocks(queries)
    moved_k = blocks(key_vectors)
    moved_v = blocks(value_vectors)
    moved_ids = image_id[inverse_place].reshape(dev_count, ROWS)
    grad_blocks = out_grad.reshape(dev_count, ROWS, D)
    grad_scale = TOKENS ** (-0.5)

    def one_device(running, items):
        query_rows, key_rows, value_rows, ids, grad_rows = items
        same_image = ids[:, None] == ids[None, :]
        attn, pullback = jax.vjp(lambda first_in, second_in, third_in: attention(first_in, second_in, third_in, same_image), query_rows, key_rows, value_rows)
        out_rows = jnp.dot(attn, out_weight, preferred_element_type=jnp.float32).astype(jnp.bfloat16)
        attn_grad = lax.dot_general(grad_rows, out_weight, (((1,), (1,)), ((), ())), preferred_element_type=jnp.float32).astype(jnp.bfloat16)
        dq_rows, dk_rows, dv_rows = pullback(attn_grad)
        term = (lax.dot_general(attn, grad_rows, (((0,), (0,)), ((), ())), preferred_element_type=jnp.float32) * grad_scale).astype(jnp.bfloat16)
        term = lax.optimization_barrier(term)
        return (running + term.astype(jnp.float32), (out_rows, dq_rows, dk_rows, dv_rows))
    start_sum = jnp.zeros((col_count, D), jnp.float32)
    summed, outputs = lax.scan(one_device, start_sum, (moved_q, moved_k, moved_v, moved_ids, grad_blocks))
    out_rows, dq_rows, dk_rows, dv_rows = outputs
    projected = out_rows.reshape(row_total, D)
    query_grad = dq_rows.reshape(row_total, col_count)[row_place]
    key_grad = dk_rows.reshape(row_total, col_count)[row_place]
    value_grad = dv_rows.reshape(row_total, col_count)[row_place]
    return (projected, query_grad, key_grad, value_grad, summed.astype(jnp.bfloat16))
```

```python
import jax
import jax.numpy as jnp
from jax import lax
from jax.sharding import PartitionSpec as P

HD = 128
SLOT = 16


def attention(query_rows, key_rows, value_rows, same_image):
    row_count = query_rows.shape[0]
    head_count = query_rows.shape[1] // HD
    query_heads = query_rows.reshape(row_count, head_count, HD).astype(jnp.float32)
    key_heads = key_rows.reshape(row_count, head_count, HD).astype(jnp.float32)
    value_heads = value_rows.reshape(row_count, head_count, HD).astype(jnp.float32)
    scores = jnp.einsum("ahd,bhd->hab", query_heads, key_heads) * HD ** (-0.5)
    scores = jnp.where(same_image[None, :, :], scores, -1e30)
    row_max = lax.stop_gradient(jnp.max(scores, axis=2, keepdims=True))
    powers = jnp.exp(scores - row_max)
    weights = (powers / jnp.sum(powers, axis=2, keepdims=True)).astype(jnp.bfloat16)
    mixed = jnp.einsum("hab,bhd->ahd", weights.astype(jnp.float32), value_heads)
    return mixed.reshape(row_count, head_count * HD).astype(jnp.bfloat16)


def select_row(table, index):
    return lax.dynamic_index_in_dim(table, index, axis=0, keepdims=False)


def take_slots(matrix, slot_source, slot_valid):
    taken = jnp.take(matrix, slot_source.reshape(-1), axis=0).reshape(
        slot_source.shape[0], slot_source.shape[1], matrix.shape[1]
    )
    return jnp.where(slot_valid[:, :, None], taken, jnp.zeros((), matrix.dtype))


def from_pool(local_rows, arrived, row_source):
    pooled = jnp.concatenate(
        [local_rows, arrived.reshape(arrived.shape[0] * arrived.shape[1], arrived.shape[2])], axis=0
    )
    return jnp.take(pooled, row_source, axis=0)


def shards(
    queries,
    key_vectors,
    value_vectors,
    image_lengths,
    image_dest,
    image_offset,
    out_weight,
    out_grad,
):
    row_count = queries.shape[0]
    img_count = image_lengths.shape[1]
    dp_count = lax.axis_size("dp")
    fs_count = lax.axis_size("fsdp")
    dp_index = lax.axis_index("dp")
    fs_index = lax.axis_index("fsdp")
    starts = jnp.cumsum(image_lengths, axis=1) - image_lengths

    def group_view(table):
        return lax.dynamic_index_in_dim(
            table.reshape(dp_count, fs_count, img_count), fs_index, axis=1, keepdims=False
        )

    grp_len = group_view(image_lengths)
    grp_start = group_view(starts)
    grp_dest = group_view(image_dest)
    grp_off = group_view(image_offset)
    own_len = select_row(grp_len, dp_index)
    own_start = select_row(grp_start, dp_index)
    own_dest = select_row(grp_dest, dp_index)
    own_off = select_row(grp_off, dp_index)
    peers = jnp.arange(dp_count, dtype=jnp.int32)
    slot_ids = jnp.arange(SLOT, dtype=jnp.int32)
    row_ids = jnp.arange(row_count, dtype=jnp.int32)
    leaving = (own_dest[None, :] == peers[:, None]) & (own_dest[None, :] != dp_index)
    send_source = (
        jnp.sum(jnp.where(leaving, own_start[None, :], 0), axis=1)[:, None] + slot_ids[None, :]
    )
    send_valid = (
        jnp.sum(
            jnp.where(
                leaving[:, :, None] & (slot_ids[None, None, :] < own_len[None, :, None]), 1, 0
            ),
            axis=1,
        )
        > 0
    )
    senders = peers[:, None]
    arriving = grp_dest == dp_index
    source_base = jnp.where(senders == dp_index, grp_start, row_count + senders * SLOT) - grp_off
    covers = (
        arriving[:, :, None]
        & (row_ids[None, None, :] >= grp_off[:, :, None])
        & (row_ids[None, None, :] < (grp_off + grp_len)[:, :, None])
    )
    row_source = jnp.sum(
        jnp.where(covers, source_base[:, :, None] + row_ids[None, None, :], 0), axis=(0, 1)
    )
    returning = arriving & (senders != dp_index)
    back_source = jnp.sum(jnp.where(returning, grp_off, 0), axis=1)[:, None] + slot_ids[None, :]
    back_valid = (
        jnp.sum(
            jnp.where(
                returning[:, :, None] & (slot_ids[None, None, :] < grp_len[:, :, None]), 1, 0
            ),
            axis=1,
        )
        > 0
    )
    stays = own_dest == dp_index
    home_base = jnp.where(stays, own_off, row_count + own_dest * SLOT) - own_start
    inside = (row_ids[None, :] >= own_start[:, None]) & (
        row_ids[None, :] < (own_start + own_len)[:, None]
    )
    home_source = jnp.sum(jnp.where(inside, home_base[:, None] + row_ids[None, :], 0), axis=0)
    segment = jnp.sum(jnp.where(row_ids[None, :] >= own_start[:, None], 1, 0), axis=0)
    home_og = lax.all_to_all(
        take_slots(out_grad, back_source, back_valid), "dp", split_axis=0, concat_axis=0, tiled=True
    )
    grad_rows = from_pool(out_grad, home_og, home_source)
    same_image = segment[:, None] == segment[None, :]
    attn, pullback = jax.vjp(
        lambda first_in, second_in, third_in: attention(first_in, second_in, third_in, same_image),
        queries,
        key_vectors,
        value_vectors,
    )
    full_weight = lax.all_gather(out_weight, "fsdp", axis=0, tiled=True)
    projected = jnp.dot(attn, full_weight, preferred_element_type=jnp.float32)
    attn_grad = lax.dot_general(
        grad_rows, full_weight, (((1,), (1,)), ((), ())), preferred_element_type=jnp.float32
    ).astype(jnp.bfloat16)
    grad_q, grad_k, grad_v = pullback(attn_grad)
    grad_scale = (row_count * dp_count * fs_count) ** (-0.5)
    weight_shard = lax.psum_scatter(
        (
            lax.dot_general(
                attn, grad_rows, (((0,), (0,)), ((), ())), preferred_element_type=jnp.float32
            )
            * grad_scale
        ).astype(jnp.bfloat16),
        "fsdp",
        scatter_dimension=0,
        tiled=True,
    )
    weight_grad = lax.psum_scatter(weight_shard, "dp", scatter_dimension=1, tiled=True)
    projected = projected.astype(jnp.bfloat16)
    got_rows = lax.all_to_all(
        take_slots(projected, send_source, send_valid), "dp", split_axis=0, concat_axis=0, tiled=True
    )
    projected = from_pool(projected, got_rows, row_source)
    return (projected, grad_q, grad_k, grad_v, weight_grad)


def solution(mesh):
    in_specs = (
        P(("dp", "fsdp"), None),
        P(("dp", "fsdp"), None),
        P(("dp", "fsdp"), None),
        P(),
        P(),
        P(),
        P("fsdp", None),
        P(("dp", "fsdp"), None),
    )
    out_specs = (
        P(("dp", "fsdp"), None),
        P(("dp", "fsdp"), None),
        P(("dp", "fsdp"), None),
        P(("dp", "fsdp"), None),
        P("fsdp", "dp"),
    )
    return jax.shard_map(shards, mesh=mesh, in_specs=in_specs, out_specs=out_specs, check_vma=False)
```

```python
import jax
import jax.numpy as jnp
from jax import lax
from jax.experimental import pallas as pl
from jax.experimental.pallas import tpu as pltpu
from jax.sharding import PartitionSpec as P

HD = 128
SLOT = 16
MESH = pl.DeviceIdType.MESH
F32 = jnp.float32
BF16 = jnp.bfloat16
ROWS = 288
D = 3072
GROUP = 768
HALF = 384
SHARD = 192
CHUNK = 48
BLOCK = 384
Z_ROWS, X_ROWS, Y_ROWS = 96, 48, 48
SCALE = HD ** (-0.5)


def flip(index, by):
    high = lax.rem(lax.div(index, 2) + by // 2, 2)
    return high * 2 + lax.rem(lax.rem(index, 2) + by % 2, 2)


def contract(first, second, first_dim, second_dim):
    return lax.dot_general(
        first, second, (((first_dim,), (second_dim,)), ((), ())), preferred_element_type=F32
    )


def kernel(
    table,
    images,
    q_hbm,
    k_hbm,
    v_hbm,
    w_hbm,
    og_hbm,
    proj_hbm,
    dq_hbm,
    dk_hbm,
    dv_hbm,
    dw_hbm,
    qv,
    kv,
    vv,
    weight,
    pool,
    og_slots,
    slot_out,
    og_pair,
    attn_half,
    attn_out,
    attn_t,
    probs,
    bias,
    heads6,
    grad_half,
    grad_out,
    grad_in,
    part,
    part_out,
    part_in,
    proj_slots,
    term_z,
    term_x,
    term_y,
    got1_z,
    got1_x,
    got1_y,
    got2_z,
    got2_x,
    got2_y,
    got3_z,
    got3_x,
    got3_y,
    dw_rows,
    load_sem,
    store_sem,
    wy_send,
    wy_recv,
    wx_send,
    wx_recv,
    a2a_send,
    a2a_recv,
    core_send,
    core_recv,
    rs_send,
    rs_recv,
):
    dp = lax.axis_index("dp")
    fs = lax.axis_index("fsdp")
    xh, z = lax.div(dp, 4), lax.rem(dp, 4)
    y, xl, core = lax.div(fs, 4), lax.rem(lax.div(fs, 2), 2), lax.rem(fs, 2)

    def device(xh_, xl_, y_, z_, core_):
        return (xh_ * 4 + z_, y_ * 4 + xl_ * 2 + core_)

    def along_x(by):
        return device(lax.rem(xh + by // 2, 2), lax.rem(xl + by % 2, 2), y, z, core)

    def along_y(by):
        return device(xh, xl, flip(y, by), z, core)

    def along_z(by):
        return device(xh, xl, y, flip(z, by), core)

    def over_dp(by):
        return device(lax.rem(xh + by // 4, 2), xl, y, flip(z, by % 4), core)

    partner = device(xh, xl, y, z, 1 - core)

    def remote(src, dst, send, recv, target):
        return pltpu.make_async_remote_copy(
            src_ref=src, dst_ref=dst, send_sem=send, recv_sem=recv, device_id=target, device_id_type=MESH
        )

    here = y * 2 + xl
    loads = [
        pltpu.make_async_copy(
            w_hbm, weight.at[pl.ds(pl.multiple_of(here * SHARD, SHARD), SHARD)], load_sem.at[0]
        ),
        pltpu.make_async_copy(og_hbm, pool.at[0:ROWS], load_sem.at[1]),
        pltpu.make_async_copy(q_hbm, qv, load_sem.at[2]),
        pltpu.make_async_copy(k_hbm, kv, load_sem.at[3]),
        pltpu.make_async_copy(v_hbm, vv, load_sem.at[4]),
    ]
    for copy in loads:
        copy.start()
    barrier = pltpu.get_barrier_semaphore()
    peers = (
        [along_x(by) for by in (1, 2, 3)]
        + [along_y(by) for by in (1, 2, 3)]
        + [along_z(by) for by in (1, 2, 3)]
        + [over_dp(by) for by in (5, 6, 7)]
        + [partner]
    )
    for peer in peers:
        pl.semaphore_signal(barrier, inc=1, device_id=peer, device_id_type=MESH)

    bias[...] = jnp.where(table[:, 2:3] == images[...], 0.0, -1e30).astype(F32)

    def pick(column, out_rows, in_rows, dst, dst_core=None):
        chosen = lax.broadcasted_iota(jnp.int32, (out_rows, in_rows), 1) == (
            table[:out_rows, column : column + 1]
        )
        one_hot = jnp.where(chosen, 1.0, 0.0).astype(BF16)

        def one_part(i, carry):
            cols = pl.ds(pl.multiple_of(i * GROUP, GROUP), GROUP)
            rows = contract(one_hot, pool[:in_rows, cols], 1, 0).astype(BF16)
            if dst_core is None:
                dst[:, cols] = rows
            else:
                dst[dst_core, :, cols] = rows
            return carry

        lax.fori_loop(0, D // GROUP, one_part, 0)

    pl.semaphore_wait(barrier, len(peers))

    def shard_rows(y_, xl_, chunk):
        return pl.ds(pl.multiple_of((y_ * 2 + xl_) * SHARD + chunk * CHUNK, CHUNK), CHUNK)

    def w_along_y(by, chunk):
        rows = weight.at[shard_rows(y, xl, chunk)]
        return remote(
            rows, rows, wy_send.at[by - 1, chunk], wy_recv.at[by - 1, chunk], along_y(by)
        )

    def w_along_x(by, chunk):
        rows = weight.at[shard_rows(flip(y, by), xl, chunk)]
        return remote(
            rows, rows, wx_send.at[by, chunk], wx_recv.at[by, chunk], along_x(1 if chunk < 2 else 3)
        )

    def forward(by, chunk):
        w_along_y(by, chunk).wait_recv()
        w_along_x(by, chunk).start()

    loads[0].wait()
    for step in range(4):
        w_along_y(1, (0, 2, 1, 3)[step]).start()
        w_along_y(3, (2, 0, 3, 1)[step]).start()
        w_along_x(0, (0, 2, 1, 3)[step]).start()

    def unit(index):
        return pl.ds(pl.multiple_of(index * SLOT, SLOT), SLOT)

    def slots(by, dst, phase):
        to_dp = lax.rem(xh + by // 4, 2) * 4 + flip(z, by % 4)
        return remote(
            slot_out.at[unit(to_dp)],
            dst.at[unit(dp)],
            a2a_send.at[phase, by - 1],
            a2a_recv.at[phase, by - 1],
            over_dp(by),
        )

    loads[1].wait()
    pick(3, 8 * SLOT, ROWS, slot_out)
    own_slot = jnp.zeros((SLOT, D), BF16)
    og_slots[unit(dp), :] = own_slot
    proj_slots[unit(dp), :] = own_slot
    for by in range(1, 8):
        slots(by, og_slots, 0).start()
    for copy in loads[2:]:
        copy.wait()

    def head_cols(head):
        return pl.ds(pl.multiple_of(head * HD, HD), HD)

    def split_cores(first, second):
        mine = jnp.where(core == 0, first, second)
        other = jnp.where(core == 0, second, first)
        return mine, other

    def attn_copy(group):
        return remote(
            attn_out.at[group],
            attn_half.at[core, group],
            core_send.at[0, group],
            core_recv.at[0, group],
            partner,
        )

    def attend(group):
        def one_head(i, carry):
            head = group * 6 + i
            cols = head_cols(head)
            scores = contract(qv[:, cols], kv[:, cols], 1, 1) * SCALE + bias[...]
            powers = jnp.exp(scores - jnp.max(scores, axis=1, keepdims=True))
            inverse = 1.0 / jnp.sum(powers, axis=1, keepdims=True)
            weights = (powers * inverse).astype(BF16)
            probs[head] = weights
            heads6[:, head_cols(i)] = contract(weights, vv[:, cols], 1, 0).astype(BF16)
            return carry

        lax.fori_loop(0, 6, one_head, 0)
        for t in range(2):
            first = heads6[:, t * HALF : t * HALF + SHARD]
            second = heads6[:, t * HALF + SHARD : (t + 1) * HALF]
            mine, other = split_cores(first, second)
            attn_half[core, group, :, t * SHARD : (t + 1) * SHARD] = mine
            attn_out[group, :, t * SHARD : (t + 1) * SHARD] = other
        attn_copy(group).start()

    attend(0)
    attend(1)
    forward(1, 0)
    forward(3, 2)
    attend(2)

    for by in range(1, 8):
        slots(by, og_slots, 0).wait_recv()
    pool[ROWS:, :] = og_slots[...]
    pick(0, ROWS, ROWS + 8 * SLOT, og_pair, core)
    og_copy = remote(
        og_pair.at[core], og_pair.at[core], core_send.at[1, 0], core_recv.at[1, 0], partner
    )
    og_copy.start()
    attend(3)
    forward(1, 2)
    forward(3, 0)
    w_along_y(2, 0).start()
    w_along_y(2, 2).start()

    for group in range(4):
        attn_copy(group).wait_recv()
        attn_t[group] = attn_half[:, group].reshape(2 * ROWS, HALF).T
    og_copy.wait_recv()

    grad_scale = (ROWS * 128) ** (-0.5)

    def copy1_z(xh_, z_, by):
        return remote(
            term_z.at[xh_, z_], got1_z.at[by - 1, xh_], rs_send.at[0, by - 1], rs_recv.at[0, by - 1],
            device(xh, xl, y, z_, core),
        )

    def copy1_x(xh_, xl_, z_, by):
        return remote(
            term_x.at[xh_, xl_, :, z_], got1_x.at[by - 1, :, z_], rs_send.at[1, by - 1],
            rs_recv.at[1, by - 1], device(xh_, xl_, y, z, core),
        )

    def copy1_y(xh_, y_, z_, by):
        return remote(
            term_y.at[y_, z_, xh_], got1_y.at[by - 1, z_, xh_], rs_send.at[2, by - 1],
            rs_recv.at[2, by - 1], device(xh, xl, y_, z, core),
        )

    def one_term(i, carry):
        by_z, by_xh = 3 - lax.div(i, 2), 1 - lax.rem(i, 2)
        z_ = lax.rem(lax.div(z, 2) + lax.div(by_z, 2), 2) * 2 + lax.rem(z + by_z, 2)
        xh_ = lax.rem(xh + by_xh, 2)
        cols = pl.ds(pl.multiple_of((xh_ * 4 + z_) * BLOCK, BLOCK), BLOCK)
        grads = og_pair[:, :, cols].reshape(2 * ROWS, BLOCK)
        for group in range(4):
            term = (contract(attn_t[group], grads, 1, 0) * grad_scale).astype(BF16)
            for xl_ in range(2):
                at = xl_ * SHARD
                term_z[xh_, z_, xl_, group] = term[at : at + Z_ROWS]
                term_x[xh_, xl_, group, z_] = term[at + Z_ROWS : at + Z_ROWS + X_ROWS]
                term_y[group, z_, xh_, xl_] = term[at + Z_ROWS + X_ROWS : at + SHARD]

        @pl.when(by_z > 0)
        def _():
            copy1_z(xh_, z_, by_z).start()

        for by_xl in range(2):

            @pl.when(by_xh * 2 + by_xl > 0)
            def _():
                copy1_x(xh_, lax.rem(xl + by_xl, 2), z_, by_xh * 2 + by_xl).start()

        for by_y in (1, 2, 3):
            copy1_y(xh_, flip(y, by_y), z_, by_y).start()
        return carry

    lax.fori_loop(0, 4, one_term, 0)
    forward(1, 1)
    forward(3, 3)
    w_along_y(2, 1).start()
    w_along_y(2, 3).start()
    lax.fori_loop(4, 8, one_term, 0)
    forward(1, 3)
    forward(3, 1)

    def grad_copy(by):
        return remote(
            grad_out.at[by], grad_in.at[by], core_send.at[2, by], core_recv.at[2, by], partner
        )

    def attn_grad(by):
        for chunk in range(4):
            w_along_x(by, chunk).wait_recv()
        rows = pl.ds(pl.multiple_of(flip(y, by) * HALF, HALF), HALF)

        def one_side(side, carry):
            owner = lax.rem(1 - core + side, 2)
            half = contract(og_pair[owner], weight[rows, :], 1, 1).astype(BF16)

            @pl.when(side == 0)
            def _():
                grad_out[by] = half

            @pl.when(side == 1)
            def _():
                grad_half[by] = half

            return carry

        one_side(0, 0)
        grad_copy(by).start()
        one_side(1, 0)

    def store_copy(by, which):
        cols = pl.ds(pl.multiple_of(flip(y, by) * GROUP, GROUP), GROUP)
        src = (qv, kv, vv)[which]
        dst = (dq_hbm, dk_hbm, dv_hbm)[which]
        return pltpu.make_async_copy(src.at[:, cols], dst.at[:, cols], store_sem.at[which, by])

    def attend_back(by):
        grad_copy(by).wait_recv()
        for t in range(2):
            mine = grad_half[by, :, t * SHARD : (t + 1) * SHARD]
            other = grad_in[by, :, t * SHARD : (t + 1) * SHARD]
            first, second = split_cores(mine, other)
            heads6[:, t * HALF : t * HALF + SHARD] = first
            heads6[:, t * HALF + SHARD : (t + 1) * HALF] = second

        def one_head(i, carry):
            head = flip(y, by) * 6 + i
            cols = head_cols(head)
            grads = heads6[:, head_cols(i)]
            weights = probs[head]
            wide = weights.astype(F32)
            queries, keys = qv[:, cols], kv[:, cols]
            products = contract(grads, vv[:, cols], 1, 1) * wide
            total = jnp.sum(products, axis=1, keepdims=True)
            score_grad = ((products - wide * total) * SCALE).astype(BF16)
            vv[:, cols] = contract(weights, grads, 0, 0).astype(BF16)
            qv[:, cols] = contract(score_grad, keys, 1, 0).astype(BF16)
            kv[:, cols] = contract(score_grad, queries, 0, 0).astype(BF16)
            return carry

        lax.fori_loop(0, 6, one_head, 0)
        for which in range(3):
            store_copy(by, which).start()

    attn_grad(0)
    attend_back(0)
    forward(2, 0)
    forward(2, 2)
    attn_grad(1)
    attend_back(1)
    forward(2, 1)
    attn_grad(3)
    forward(2, 3)
    attend_back(3)
    attn_grad(2)

    def part_copy(block):
        return remote(
            part_out.at[block], part_in.at[block], core_send.at[3, block], core_recv.at[3, block],
            partner,
        )

    def one_block(block, carry):
        cols = pl.ds(pl.multiple_of(block * BLOCK, BLOCK), BLOCK)
        total = jnp.zeros((2 * ROWS, BLOCK), F32)
        for group in range(4):
            total += contract(
                attn_half[:, group].reshape(2 * ROWS, HALF),
                weight[group * HALF : (group + 1) * HALF, cols],
                1,
                0,
            )
        part[...] = total.reshape(2, ROWS, BLOCK)
        part_out[block] = part[1 - core].astype(BF16)
        part_copy(block).start()
        pool[:ROWS, cols] = part[core].astype(BF16)
        return carry

    lax.fori_loop(0, 8, one_block, 0)

    def add_block(block, carry):
        cols = pl.ds(pl.multiple_of(block * BLOCK, BLOCK), BLOCK)
        part_copy(block).wait_recv()
        pool[:ROWS, cols] = (
            pool[:ROWS, cols].astype(F32) + part_in[block].astype(F32)
        ).astype(BF16)
        return carry

    lax.fori_loop(0, 8, add_block, 0)

    for by in range(1, 8):
        slots(by, og_slots, 0).wait_send()
    pick(4, 8 * SLOT, ROWS, slot_out)
    for by in range(1, 8):
        slots(by, proj_slots, 1).start()

    attend_back(2)

    def all_of(buffer, sem):
        return pltpu.make_async_copy(buffer, buffer, sem)

    def summed(own, others):
        total = own.astype(F32)
        for other in others:
            total += other.astype(F32)
        return total

    def wait_got(buffer, kind):
        for by in (1, 2, 3):
            all_of(buffer.at[by - 1], rs_recv.at[kind, by - 1]).wait()

    wait_got(got1_z, 0)

    def sum1_z(i, carry):
        xh_, xl_, y_ = lax.div(i, 8), lax.rem(lax.div(i, 4), 2), lax.rem(i, 4)
        term_z[xh_, z, xl_, y_] = summed(
            term_z[xh_, z, xl_, y_], [got1_z[r, xh_, xl_, y_] for r in range(3)]
        ).astype(BF16)
        return carry

    lax.fori_loop(0, 16, sum1_z, 0)

    def copy2_z(by):
        xh_, xl_ = lax.rem(xh + by // 2, 2), lax.rem(xl + by % 2, 2)
        return remote(
            term_z.at[xh_, z, xl_], got2_z.at[by - 1], rs_send.at[3, by - 1], rs_recv.at[3, by - 1],
            along_x(by),
        )

    for by in (1, 2, 3):
        copy2_z(by).start()

    wait_got(got1_x, 1)

    def sum1_x(i, carry):
        y_, z_ = lax.div(i, 4), lax.rem(i, 4)
        term_x[xh, xl, y_, z_] = summed(
            term_x[xh, xl, y_, z_], [got1_x[r, y_, z_] for r in range(3)]
        ).astype(BF16)
        return carry

    lax.fori_loop(0, 16, sum1_x, 0)

    def copy2_x(by):
        return remote(
            term_x.at[xh, xl, flip(y, by)], got2_x.at[by - 1], rs_send.at[4, by - 1],
            rs_recv.at[4, by - 1], along_y(by),
        )

    for by in (1, 2, 3):
        copy2_x(by).start()

    wait_got(got1_y, 2)

    def sum1_y(i, carry):
        z_, xh_, xl_ = lax.div(i, 4), lax.rem(lax.div(i, 2), 2), lax.rem(i, 2)
        term_y[y, z_, xh_, xl_] = summed(
            term_y[y, z_, xh_, xl_], [got1_y[r, z_, xh_, xl_] for r in range(3)]
        ).astype(BF16)
        return carry

    lax.fori_loop(0, 16, sum1_y, 0)

    def copy2_y(by):
        return remote(
            term_y.at[y, flip(z, by)], got2_y.at[by - 1], rs_send.at[5, by - 1],
            rs_recv.at[5, by - 1], along_z(by),
        )

    for by in (1, 2, 3):
        copy2_y(by).start()

    for by in range(1, 8):
        slots(by, proj_slots, 1).wait_recv()
    pool[ROWS:, :] = proj_slots[...]
    og_copy.wait_send()
    pick(1, ROWS, ROWS + 8 * SLOT, og_pair, core)
    proj_copy = pltpu.make_async_copy(og_pair.at[core], proj_hbm, load_sem.at[0])
    proj_copy.start()

    wait_got(got2_x, 4)
    for z_ in range(4):
        term_x[xh, xl, y, z_] = summed(
            term_x[xh, xl, y, z_], [got2_x[r, z_] for r in range(3)]
        ).astype(BF16)

    def copy3_x(by):
        return remote(
            term_x.at[xh, xl, y, flip(z, by)], got3_x.at[by - 1], rs_send.at[6, by - 1],
            rs_recv.at[6, by - 1], along_z(by),
        )

    for by in (1, 2, 3):
        copy3_x(by).start()

    wait_got(got2_y, 5)
    for xh_ in range(2):
        for xl_ in range(2):
            term_y[y, z, xh_, xl_] = summed(
                term_y[y, z, xh_, xl_], [got2_y[r, xh_, xl_] for r in range(3)]
            ).astype(BF16)

    def copy3_y(by):
        return remote(
            term_y.at[y, z, lax.rem(xh + by // 2, 2), lax.rem(xl + by % 2, 2)], got3_y.at[by - 1],
            rs_send.at[7, by - 1], rs_recv.at[7, by - 1], along_x(by),
        )

    for by in (1, 2, 3):
        copy3_y(by).start()

    wait_got(got2_z, 3)
    for y_ in range(4):
        term_z[xh, z, xl, y_] = summed(
            term_z[xh, z, xl, y_], [got2_z[r, y_] for r in range(3)]
        ).astype(BF16)

    def copy3_z(by):
        return remote(
            term_z.at[xh, z, xl, flip(y, by)], got3_z.at[by - 1], rs_send.at[8, by - 1],
            rs_recv.at[8, by - 1], along_y(by),
        )

    for by in (1, 2, 3):
        copy3_z(by).start()

    wait_got(got3_x, 6)
    dw_rows[Z_ROWS : Z_ROWS + X_ROWS, :] = summed(
        term_x[xh, xl, y, z], [got3_x[r] for r in range(3)]
    ).astype(BF16)
    wait_got(got3_y, 7)
    dw_rows[Z_ROWS + X_ROWS :, :] = summed(
        term_y[y, z, xh, xl], [got3_y[r] for r in range(3)]
    ).astype(BF16)
    wait_got(got3_z, 8)
    dw_rows[:Z_ROWS, :] = summed(term_z[xh, z, xl, y], [got3_z[r] for r in range(3)]).astype(BF16)
    dw_copy = pltpu.make_async_copy(dw_rows, dw_hbm, load_sem.at[1])
    dw_copy.start()

    for by in range(4):
        for chunk in range(4):
            if by > 0:
                w_along_y(by, chunk).wait_send()
            w_along_x(by, chunk).wait_send()
        attn_copy(by).wait_send()
        grad_copy(by).wait_send()
    for by in range(1, 8):
        slots(by, proj_slots, 1).wait_send()
    for block in range(8):
        part_copy(block).wait_send()
    sent = (got1_z, got1_x, got1_y, got2_z, got2_x, got2_y, got3_x, got3_y, got3_z)
    for kind in range(9):
        for by in (1, 2, 3):
            all_of(sent[kind].at[by - 1], rs_send.at[kind, by - 1]).wait()
    for by in range(4):
        for which in range(3):
            store_copy(by, which).wait()
    proj_copy.wait()
    dw_copy.wait()


def row_tables(image_lengths, image_dest, image_offset):
    img_count = image_lengths.shape[1]
    dp_count = lax.axis_size("dp")
    fs_count = lax.axis_size("fsdp")
    dp_index = lax.axis_index("dp")
    fs_index = lax.axis_index("fsdp")
    starts = jnp.cumsum(image_lengths, axis=1) - image_lengths

    def group_view(table):
        return lax.dynamic_index_in_dim(
            table.reshape(dp_count, fs_count, img_count), fs_index, axis=1, keepdims=False
        )

    def own(table):
        return lax.dynamic_index_in_dim(table, dp_index, axis=0, keepdims=False)

    grp_len = group_view(image_lengths) // SLOT
    grp_start = group_view(starts) // SLOT
    grp_dest = group_view(image_dest)
    grp_off = group_view(image_offset) // SLOT
    own_len, own_start, own_dest, own_off = own(grp_len), own(grp_start), own(grp_dest), own(grp_off)
    peers = jnp.arange(dp_count, dtype=jnp.int32)
    unit_count = ROWS // SLOT
    units = jnp.arange(unit_count, dtype=jnp.int32)
    arriving = grp_dest == dp_index
    senders = peers[:, None]
    back = jnp.sum(jnp.where(arriving & (senders != dp_index), grp_off, 0), axis=1)
    home_base = jnp.where(own_dest == dp_index, own_off, unit_count + own_dest) - own_start
    inside = (units[None, :] >= own_start[:, None]) & (units[None, :] < (own_start + own_len)[:, None])
    home = jnp.sum(jnp.where(inside, home_base[:, None] + units[None, :], 0), axis=0)
    leaving = (own_dest[None, :] == peers[:, None]) & (own_dest[None, :] != dp_index)
    send = jnp.sum(jnp.where(leaving, own_start[None, :], 0), axis=1)
    source_base = jnp.where(senders == dp_index, grp_start, unit_count + senders) - grp_off
    covers = (
        arriving[:, :, None]
        & (units[None, None, :] >= grp_off[:, :, None])
        & (units[None, None, :] < (grp_off + grp_len)[:, :, None])
    )
    place = jnp.sum(
        jnp.where(covers, source_base[:, :, None] + units[None, None, :], 0), axis=(0, 1)
    )
    within = jnp.arange(SLOT, dtype=jnp.int32)

    def unit_rows(first):
        return (first[:, None] * SLOT + within[None, :]).reshape(-1)

    row_ids = jnp.arange(ROWS, dtype=jnp.int32)
    image = jnp.sum(jnp.where(row_ids[None, :] >= (own_start * SLOT)[:, None], 1, 0), axis=0)
    fill = (0, ROWS - dp_count * SLOT)
    columns = [
        unit_rows(home),
        unit_rows(place),
        image,
        jnp.pad(unit_rows(back), fill),
        jnp.pad(unit_rows(send), fill),
    ]
    return jnp.stack(columns, axis=1).astype(jnp.int32), image[None, :].astype(jnp.int32)


def shards(
    queries, key_vectors, value_vectors, image_lengths, image_dest, image_offset, out_weight, out_grad
):
    table, images = row_tables(image_lengths, image_dest, image_offset)
    any_space = pl.BlockSpec(memory_space=pl.ANY)
    rows = jax.ShapeDtypeStruct((ROWS, D), BF16)
    vmem = pltpu.VMEM
    dma = pltpu.SemaphoreType.DMA
    return pl.pallas_call(
        kernel,
        out_shape=(rows, rows, rows, rows, jax.ShapeDtypeStruct((SHARD, BLOCK), BF16)),
        in_specs=[pl.BlockSpec(memory_space=vmem)] * 2 + [any_space] * 5,
        out_specs=[any_space] * 5,
        scratch_shapes=[
            vmem((ROWS, D), BF16),
            vmem((ROWS, D), BF16),
            vmem((ROWS, D), BF16),
            vmem((8 * SHARD, D), BF16),
            vmem((ROWS + 8 * SLOT, D), BF16),
            vmem((8 * SLOT, D), BF16),
            vmem((8 * SLOT, D), BF16),
            vmem((2, ROWS, D), BF16),
            vmem((2, 4, ROWS, HALF), BF16),
            vmem((4, ROWS, HALF), BF16),
            vmem((4, HALF, 2 * ROWS), BF16),
            vmem((24, ROWS, ROWS), BF16),
            vmem((ROWS, ROWS), F32),
            vmem((ROWS, GROUP), BF16),
            vmem((4, ROWS, HALF), BF16),
            vmem((4, ROWS, HALF), BF16),
            vmem((4, ROWS, HALF), BF16),
            vmem((2, ROWS, BLOCK), F32),
            vmem((8, ROWS, BLOCK), BF16),
            vmem((8, ROWS, BLOCK), BF16),
            vmem((8 * SLOT, D), BF16),
            vmem((2, 4, 2, 4, Z_ROWS, BLOCK), BF16),
            vmem((2, 2, 4, 4, X_ROWS, BLOCK), BF16),
            vmem((4, 4, 2, 2, Y_ROWS, BLOCK), BF16),
            vmem((3, 2, 2, 4, Z_ROWS, BLOCK), BF16),
            vmem((3, 4, 4, X_ROWS, BLOCK), BF16),
            vmem((3, 4, 2, 2, Y_ROWS, BLOCK), BF16),
            vmem((3, 4, Z_ROWS, BLOCK), BF16),
            vmem((3, 4, X_ROWS, BLOCK), BF16),
            vmem((3, 2, 2, Y_ROWS, BLOCK), BF16),
            vmem((3, Z_ROWS, BLOCK), BF16),
            vmem((3, X_ROWS, BLOCK), BF16),
            vmem((3, Y_ROWS, BLOCK), BF16),
            vmem((SHARD, BLOCK), BF16),
            dma((5,)),
            dma((3, 4)),
            dma((3, 4)),
            dma((3, 4)),
            dma((4, 4)),
            dma((4, 4)),
            dma((2, 7)),
            dma((2, 7)),
            dma((4, 8)),
            dma((4, 8)),
            dma((9, 3)),
            dma((9, 3)),
        ],
        compiler_params=pltpu.CompilerParams(
            collective_id=0, has_side_effects=True, vmem_limit_bytes=63 * 2**20
        ),
        name="attention_step",
    )(table, images, queries, key_vectors, value_vectors, out_weight, out_grad)


def solution(mesh):
    rows = P(("dp", "fsdp"), None)
    return jax.shard_map(
        shards,
        mesh=mesh,
        in_specs=(rows, rows, rows, P(), P(), P(), P("fsdp", None), rows),
        out_specs=(rows, rows, rows, rows, P("fsdp", "dp")),
        check_vma=False,
    )
```

```python
import jax
import jax.numpy as jnp
from jax import lax
from jax.experimental import pallas as pl
from jax.experimental.pallas import tpu as pltpu
from jax.sharding import PartitionSpec as P

HD = 128
SLOT = 16
MESH = pl.DeviceIdType.MESH
F32 = jnp.float32
BF16 = jnp.bfloat16
ROWS = 288
D = 3072
GROUP = 768
HALF = 384
SHARD = 192
CHUNK = 48
BLOCK = 384
PIPES = ((0, 64, "zyx", 1), (64, 64, "zxy", 3), (128, 32, "yzx", 1), (160, 32, "yxz", 3))
SCALE = HD ** (-0.5)


def flip(index, by):
    high = lax.rem(lax.div(index, 2) + by // 2, 2)
    return high * 2 + lax.rem(lax.rem(index, 2) + by % 2, 2)


def contract(first, second, first_dim, second_dim):
    return lax.dot_general(
        first, second, (((first_dim,), (second_dim,)), ((), ())), preferred_element_type=F32
    )


def kernel(
    table,
    images,
    q_hbm,
    k_hbm,
    v_hbm,
    w_hbm,
    og_hbm,
    proj_hbm,
    dq_hbm,
    dk_hbm,
    dv_hbm,
    dw_hbm,
    qv,
    kv,
    vv,
    weight,
    pool,
    og_slots,
    slot_out,
    og_pair,
    attn_half,
    attn_out,
    attn_t,
    probs,
    bias,
    heads6,
    grad_half,
    grad_out,
    grad_in,
    part,
    part_out,
    part_in,
    proj_slots,
    term_0,
    term_1,
    term_2,
    term_3,
    pair_0,
    pair_1,
    pair_2,
    pair_3,
    quad_0,
    quad_1,
    quad_2,
    quad_3,
    next_0,
    next_1,
    next_2,
    next_3,
    last_0,
    last_1,
    last_2,
    last_3,
    dw_rows,
    load_sem,
    store_sem,
    wy_send,
    wy_recv,
    wx_send,
    wx_recv,
    a2a_send,
    a2a_recv,
    core_send,
    core_recv,
    rs_send,
    rs_recv,
):
    dp = lax.axis_index("dp")
    fs = lax.axis_index("fsdp")
    xh, z = lax.div(dp, 4), lax.rem(dp, 4)
    y, xl, core = lax.div(fs, 4), lax.rem(lax.div(fs, 2), 2), lax.rem(fs, 2)

    def device(xh_, xl_, y_, z_, core_):
        return (xh_ * 4 + z_, y_ * 4 + xl_ * 2 + core_)

    def along_x(by):
        return device(lax.rem(xh + by // 2, 2), lax.rem(xl + by % 2, 2), y, z, core)

    def along_y(by):
        return device(xh, xl, flip(y, by), z, core)

    def along_z(by):
        return device(xh, xl, y, flip(z, by), core)

    def over_dp(by):
        return device(lax.rem(xh + by // 4, 2), xl, y, flip(z, by % 4), core)

    partner = device(xh, xl, y, z, 1 - core)

    def remote(src, dst, send, recv, target):
        return pltpu.make_async_remote_copy(
            src_ref=src, dst_ref=dst, send_sem=send, recv_sem=recv, device_id=target, device_id_type=MESH
        )

    here = y * 2 + xl
    loads = [
        pltpu.make_async_copy(
            w_hbm, weight.at[pl.ds(pl.multiple_of(here * SHARD, SHARD), SHARD)], load_sem.at[0]
        ),
        pltpu.make_async_copy(og_hbm, pool.at[0:ROWS], load_sem.at[1]),
        pltpu.make_async_copy(q_hbm, qv, load_sem.at[2]),
        pltpu.make_async_copy(k_hbm, kv, load_sem.at[3]),
        pltpu.make_async_copy(v_hbm, vv, load_sem.at[4]),
    ]
    for copy in loads:
        copy.start()
    barrier = pltpu.get_barrier_semaphore()
    peers = (
        [along_x(by) for by in (1, 2, 3)]
        + [along_y(by) for by in (1, 2, 3)]
        + [along_z(by) for by in (1, 2, 3)]
        + [over_dp(by) for by in (5, 6, 7)]
        + [partner]
    )
    for peer in peers:
        pl.semaphore_signal(barrier, inc=1, device_id=peer, device_id_type=MESH)

    bias[...] = jnp.where(table[:, 2:3] == images[...], 0.0, -1e30).astype(F32)

    def pick(column, out_rows, in_rows, dst, dst_core=None):
        chosen = lax.broadcasted_iota(jnp.int32, (out_rows, in_rows), 1) == (
            table[:out_rows, column : column + 1]
        )
        one_hot = jnp.where(chosen, 1.0, 0.0).astype(BF16)

        def one_part(i, carry):
            cols = pl.ds(pl.multiple_of(i * GROUP, GROUP), GROUP)
            rows = contract(one_hot, pool[:in_rows, cols], 1, 0).astype(BF16)
            if dst_core is None:
                dst[:, cols] = rows
            else:
                dst[dst_core, :, cols] = rows
            return carry

        lax.fori_loop(0, D // GROUP, one_part, 0)

    pl.semaphore_wait(barrier, len(peers))

    def shard_rows(y_, xl_, chunk):
        return pl.ds(pl.multiple_of((y_ * 2 + xl_) * SHARD + chunk * CHUNK, CHUNK), CHUNK)

    def w_along_y(by, chunk):
        via = (1 if chunk < 2 else 3) if by == 2 else 0
        rows = weight.at[shard_rows(flip(y, via), xl, chunk)]
        return remote(
            rows,
            rows,
            wy_send.at[by - 1, chunk],
            wy_recv.at[by - 1, chunk],
            along_y(4 - via if by == 2 else by),
        )

    def w_along_x(by, chunk):
        rows = weight.at[shard_rows(flip(y, by), xl, chunk)]
        return remote(
            rows,
            rows,
            wx_send.at[by, chunk],
            wx_recv.at[by, chunk],
            along_x(1 if chunk % 2 == 0 else 3),
        )

    def forward(by, chunk):
        w_along_y(by, chunk).wait_recv()
        if by == (1 if chunk < 2 else 3):
            w_along_y(2, chunk).start()
        w_along_x(by, chunk).start()

    loads[0].wait()
    for step in range(4):
        w_along_y(1, step).start()
        w_along_y(3, 3 - step).start()
        w_along_x(0, step).start()

    def unit(index):
        return pl.ds(pl.multiple_of(index * SLOT, SLOT), SLOT)

    def slots(by, dst, phase):
        to_dp = lax.rem(xh + by // 4, 2) * 4 + flip(z, by % 4)
        return remote(
            slot_out.at[unit(to_dp)],
            dst.at[unit(dp)],
            a2a_send.at[phase, by - 1],
            a2a_recv.at[phase, by - 1],
            over_dp(by),
        )

    loads[1].wait()
    pick(3, 8 * SLOT, ROWS, slot_out)
    own_slot = jnp.zeros((SLOT, D), BF16)
    og_slots[unit(dp), :] = own_slot
    proj_slots[unit(dp), :] = own_slot
    for by in range(1, 8):
        slots(by, og_slots, 0).start()
    for copy in loads[2:]:
        copy.wait()

    def head_cols(head):
        return pl.ds(pl.multiple_of(head * HD, HD), HD)

    def split_cores(first, second):
        mine = jnp.where(core == 0, first, second)
        other = jnp.where(core == 0, second, first)
        return mine, other

    def attn_copy(group):
        return remote(
            attn_out.at[group],
            attn_half.at[core, group],
            core_send.at[0, group],
            core_recv.at[0, group],
            partner,
        )

    def attend(group):
        def one_head(i, carry):
            head = group * 6 + i
            cols = head_cols(head)
            scores = contract(qv[:, cols], kv[:, cols], 1, 1) * SCALE + bias[...]
            powers = jnp.exp(scores - jnp.max(scores, axis=1, keepdims=True))
            inverse = 1.0 / jnp.sum(powers, axis=1, keepdims=True)
            weights = (powers * inverse).astype(BF16)
            probs[head] = weights
            heads6[:, head_cols(i)] = contract(weights, vv[:, cols], 1, 0).astype(BF16)
            return carry

        lax.fori_loop(0, 6, one_head, 0)
        for t in range(2):
            first = heads6[:, t * HALF : t * HALF + SHARD]
            second = heads6[:, t * HALF + SHARD : (t + 1) * HALF]
            mine, other = split_cores(first, second)
            attn_half[core, group, :, t * SHARD : (t + 1) * SHARD] = mine
            attn_out[group, :, t * SHARD : (t + 1) * SHARD] = other
        attn_copy(group).start()

    attend(0)
    attend(1)
    forward(1, 0)
    forward(3, 3)
    attend(2)

    for by in range(1, 8):
        slots(by, og_slots, 0).wait_recv()
    pool[ROWS:, :] = og_slots[...]
    pick(0, ROWS, ROWS + 8 * SLOT, og_pair, core)
    og_copy = remote(
        og_pair.at[core], og_pair.at[core], core_send.at[1, 0], core_recv.at[1, 0], partner
    )
    og_copy.start()
    attend(3)
    forward(1, 1)
    forward(3, 2)

    for group in range(4):
        attn_copy(group).wait_recv()
        attn_t[group] = attn_half[:, group].reshape(2 * ROWS, HALF).T
    og_copy.wait_recv()

    grad_scale = (ROWS * 128) ** (-0.5)

    x = xh * 2 + xl
    here_on = {"x": x, "y": y, "z": z}
    along = {"x": along_x, "y": along_y, "z": along_z}
    terms = (term_0, term_1, term_2, term_3)
    pairs = (pair_0, pair_1, pair_2, pair_3)
    quads = (quad_0, quad_1, quad_2, quad_3)
    nexts = (next_0, next_1, next_2, next_3)
    lasts = (last_0, last_1, last_2, last_3)

    def first_copy(pipe, by, z_):
        near = PIPES[pipe][3]
        slot = 0 if by == 2 else 1
        term, pair = terms[pipe], pairs[pipe].at[slot]
        if pipe < 2:
            src, dst = term.at[z_], pair
        elif pipe == 2:
            src, dst = term.at[flip(y, by), z_], pair.at[z_]
        else:
            src, dst = term.at[flip(y, by), :, z_], pair.at[:, z_]
        return remote(
            src, dst, rs_send.at[pipe, slot], rs_recv.at[pipe, slot], along[PIPES[pipe][2][0]](near)
        )

    def compute_terms(by_z):
        z_ = flip(z, by_z)

        def one_term(by_xh, carry):
            xh_ = lax.rem(xh + 1 + by_xh, 2)
            cols = pl.ds(pl.multiple_of((xh_ * 4 + z_) * BLOCK, BLOCK), BLOCK)
            grads = og_pair[:, :, cols].reshape(2 * ROWS, BLOCK)
            for y_ in range(4):
                term = (contract(attn_t[y_], grads, 1, 0) * grad_scale).astype(BF16)
                for xl_ in range(2):
                    x_ = xh_ * 2 + xl_
                    places = ((z_, y_, x_), (z_, x_, y_), (y_, z_, x_), (y_, x_, z_))
                    for (first_row, count, _, _), buffer, place in zip(PIPES, terms, places):
                        at = xl_ * SHARD + first_row
                        buffer[place] = term[at : at + count]
            return carry

        lax.fori_loop(0, 2, one_term, 0)
        for pipe in range(4):
            near = PIPES[pipe][3]
            if pipe < 2:
                if by_z in (2, near):
                    first_copy(pipe, by_z, z_).start()
            else:
                first_copy(pipe, 2, z_).start()
                first_copy(pipe, near, z_).start()

    compute_terms(2)
    forward(1, 2)
    forward(3, 1)
    compute_terms(1)
    compute_terms(3)
    forward(1, 3)
    forward(3, 0)
    compute_terms(0)

    def grad_copy(by):
        return remote(
            grad_out.at[by], grad_in.at[by], core_send.at[2, by], core_recv.at[2, by], partner
        )

    def attn_grad(by):
        for chunk in range(4):
            w_along_x(by, chunk).wait_recv()
        rows = pl.ds(pl.multiple_of(flip(y, by) * HALF, HALF), HALF)

        def one_side(side, carry):
            owner = lax.rem(1 - core + side, 2)
            half = contract(og_pair[owner], weight[rows, :], 1, 1).astype(BF16)

            @pl.when(side == 0)
            def _():
                grad_out[by] = half

            @pl.when(side == 1)
            def _():
                grad_half[by] = half

            return carry

        one_side(0, 0)
        grad_copy(by).start()
        one_side(1, 0)

    def store_copy(by, which):
        cols = pl.ds(pl.multiple_of(flip(y, by) * GROUP, GROUP), GROUP)
        src = (qv, kv, vv)[which]
        dst = (dq_hbm, dk_hbm, dv_hbm)[which]
        return pltpu.make_async_copy(src.at[:, cols], dst.at[:, cols], store_sem.at[which, by])

    def attend_back(by):
        grad_copy(by).wait_recv()
        for t in range(2):
            mine = grad_half[by, :, t * SHARD : (t + 1) * SHARD]
            other = grad_in[by, :, t * SHARD : (t + 1) * SHARD]
            first, second = split_cores(mine, other)
            heads6[:, t * HALF : t * HALF + SHARD] = first
            heads6[:, t * HALF + SHARD : (t + 1) * HALF] = second

        def one_head(i, carry):
            head = flip(y, by) * 6 + i
            cols = head_cols(head)
            grads = heads6[:, head_cols(i)]
            weights = probs[head]
            wide = weights.astype(F32)
            queries, keys = qv[:, cols], kv[:, cols]
            products = contract(grads, vv[:, cols], 1, 1) * wide
            total = jnp.sum(products, axis=1, keepdims=True)
            score_grad = ((products - wide * total) * SCALE).astype(BF16)
            vv[:, cols] = contract(weights, grads, 0, 0).astype(BF16)
            qv[:, cols] = contract(score_grad, keys, 1, 0).astype(BF16)
            kv[:, cols] = contract(score_grad, queries, 0, 0).astype(BF16)
            return carry

        lax.fori_loop(0, 6, one_head, 0)
        for which in range(3):
            store_copy(by, which).start()

    def all_of(buffer, sem):
        return pltpu.make_async_copy(buffer, buffer, sem)

    def summed(own, others):
        total = own.astype(F32)
        for other in others:
            total += other.astype(F32)
        return total.astype(BF16)

    def second_copy(pipe, half):
        _, _, axes, near = PIPES[pipe]
        rows = pl.ds(half * 2, 2)
        return remote(
            terms[pipe].at[flip(here_on[axes[0]], 4 - near), rows],
            quads[pipe].at[rows],
            rs_send.at[pipe, 2],
            rs_recv.at[pipe, 2],
            along[axes[0]](4 - near),
        )

    def pipe_second(pipe):
        term, pair = terms[pipe], pairs[pipe]
        far = flip(here_on[PIPES[pipe][2][0]], 4 - PIPES[pipe][3])
        all_of(pair.at[0], rs_recv.at[pipe, 0]).wait()
        for half in range(2):

            def one_block(i, carry):
                second, third = half * 2 + lax.div(i, 4), lax.rem(i, 4)
                term[far, second, third] = summed(
                    term[far, second, third], [pair[0, second, third]]
                )
                return carry

            lax.fori_loop(0, 8, one_block, 0)
            second_copy(pipe, half).start()

    def third_copy(pipe, by):
        axes = PIPES[pipe][2]
        return remote(
            terms[pipe].at[here_on[axes[0]], flip(here_on[axes[1]], by)],
            nexts[pipe].at[by - 1],
            rs_send.at[pipe, 2 + by],
            rs_recv.at[pipe, 2 + by],
            along[axes[1]](by),
        )

    def pipe_third(pipe):
        term, pair, quad = terms[pipe], pairs[pipe], quads[pipe]
        own = here_on[PIPES[pipe][2][0]]
        all_of(pair.at[1], rs_recv.at[pipe, 1]).wait()
        all_of(quad, rs_recv.at[pipe, 2]).wait()

        def one_block(i, carry):
            second, third = lax.div(i, 4), lax.rem(i, 4)
            term[own, second, third] = summed(
                term[own, second, third], [pair[1, second, third], quad[second, third]]
            )
            return carry

        lax.fori_loop(0, 16, one_block, 0)
        for by in (2, 1, 3):
            third_copy(pipe, by).start()

    def fourth_copy(pipe, by):
        axes = PIPES[pipe][2]
        return remote(
            terms[pipe].at[here_on[axes[0]], here_on[axes[1]], flip(here_on[axes[2]], by)],
            lasts[pipe].at[by - 1],
            rs_send.at[pipe, 5 + by],
            rs_recv.at[pipe, 5 + by],
            along[axes[2]](by),
        )

    def pipe_fourth(pipe):
        term, arrived = terms[pipe], nexts[pipe]
        axes = PIPES[pipe][2]
        own = here_on[axes[0]], here_on[axes[1]]
        for by in (1, 2, 3):
            third_copy(pipe, by).wait_recv()

        def one_block(third, carry):
            place = own + (third,)
            term[place] = summed(term[place], [arrived[r, third] for r in range(3)])
            return carry

        lax.fori_loop(0, 4, one_block, 0)
        for by in (2, 1, 3):
            fourth_copy(pipe, by).start()

    def pipe_last(pipe):
        first_row, count, axes, _ = PIPES[pipe]
        for by in (1, 2, 3):
            fourth_copy(pipe, by).wait_recv()
        dw_rows[first_row : first_row + count, :] = summed(
            terms[pipe][tuple(here_on[axis] for axis in axes)], [lasts[pipe][r] for r in range(3)]
        )

    attn_grad(0)
    attend_back(0)
    forward(2, 0)
    forward(2, 3)
    attn_grad(1)
    attend_back(1)
    forward(2, 1)
    forward(2, 2)
    pipe_second(0)
    pipe_second(1)
    attn_grad(3)
    attend_back(3)
    pipe_second(2)
    pipe_second(3)
    attn_grad(2)

    def part_copy(block):
        return remote(
            part_out.at[block], part_in.at[block], core_send.at[3, block], core_recv.at[3, block],
            partner,
        )

    def one_block(block, carry):
        cols = pl.ds(pl.multiple_of(block * BLOCK, BLOCK), BLOCK)
        total = jnp.zeros((2 * ROWS, BLOCK), F32)
        for group in range(4):
            total += contract(
                attn_half[:, group].reshape(2 * ROWS, HALF),
                weight[group * HALF : (group + 1) * HALF, cols],
                1,
                0,
            )
        part[...] = total.reshape(2, ROWS, BLOCK)
        part_out[block] = part[1 - core].astype(BF16)
        part_copy(block).start()
        pool[:ROWS, cols] = part[core].astype(BF16)
        return carry

    lax.fori_loop(0, 8, one_block, 0)

    def add_block(block, carry):
        cols = pl.ds(pl.multiple_of(block * BLOCK, BLOCK), BLOCK)
        part_copy(block).wait_recv()
        pool[:ROWS, cols] = (
            pool[:ROWS, cols].astype(F32) + part_in[block].astype(F32)
        ).astype(BF16)
        return carry

    lax.fori_loop(0, 8, add_block, 0)

    for by in range(1, 8):
        slots(by, og_slots, 0).wait_send()
    pick(4, 8 * SLOT, ROWS, slot_out)
    for by in range(1, 8):
        slots(by, proj_slots, 1).start()

    attend_back(2)

    for pipe in (2, 3, 0, 1):
        pipe_third(pipe)

    for by in range(1, 8):
        slots(by, proj_slots, 1).wait_recv()
    pool[ROWS:, :] = proj_slots[...]
    og_copy.wait_send()
    pick(1, ROWS, ROWS + 8 * SLOT, og_pair, core)
    proj_copy = pltpu.make_async_copy(og_pair.at[core], proj_hbm, load_sem.at[0])
    proj_copy.start()

    for pipe in (2, 3, 0, 1):
        pipe_fourth(pipe)
    for pipe in (2, 3, 0, 1):
        pipe_last(pipe)
    dw_copy = pltpu.make_async_copy(dw_rows, dw_hbm, load_sem.at[1])
    dw_copy.start()

    for by in range(4):
        for chunk in range(4):
            if by > 0:
                w_along_y(by, chunk).wait_send()
            w_along_x(by, chunk).wait_send()
        attn_copy(by).wait_send()
        grad_copy(by).wait_send()
    for by in range(1, 8):
        slots(by, proj_slots, 1).wait_send()
    for block in range(8):
        part_copy(block).wait_send()
    for pipe in range(4):
        for slot in range(2):
            all_of(pairs[pipe].at[slot], rs_send.at[pipe, slot]).wait()
        all_of(quads[pipe], rs_send.at[pipe, 2]).wait()
        for by in (1, 2, 3):
            third_copy(pipe, by).wait_send()
            fourth_copy(pipe, by).wait_send()
    for by in range(4):
        for which in range(3):
            store_copy(by, which).wait()
    proj_copy.wait()
    dw_copy.wait()


def row_tables(image_lengths, image_dest, image_offset):
    img_count = image_lengths.shape[1]
    dp_count = lax.axis_size("dp")
    fs_count = lax.axis_size("fsdp")
    dp_index = lax.axis_index("dp")
    fs_index = lax.axis_index("fsdp")
    starts = jnp.cumsum(image_lengths, axis=1) - image_lengths

    def group_view(table):
        return lax.dynamic_index_in_dim(
            table.reshape(dp_count, fs_count, img_count), fs_index, axis=1, keepdims=False
        )

    def own(table):
        return lax.dynamic_index_in_dim(table, dp_index, axis=0, keepdims=False)

    grp_len = group_view(image_lengths) // SLOT
    grp_start = group_view(starts) // SLOT
    grp_dest = group_view(image_dest)
    grp_off = group_view(image_offset) // SLOT
    own_len, own_start, own_dest, own_off = own(grp_len), own(grp_start), own(grp_dest), own(grp_off)
    peers = jnp.arange(dp_count, dtype=jnp.int32)
    unit_count = ROWS // SLOT
    units = jnp.arange(unit_count, dtype=jnp.int32)
    arriving = grp_dest == dp_index
    senders = peers[:, None]
    back = jnp.sum(jnp.where(arriving & (senders != dp_index), grp_off, 0), axis=1)
    home_base = jnp.where(own_dest == dp_index, own_off, unit_count + own_dest) - own_start
    inside = (units[None, :] >= own_start[:, None]) & (units[None, :] < (own_start + own_len)[:, None])
    home = jnp.sum(jnp.where(inside, home_base[:, None] + units[None, :], 0), axis=0)
    leaving = (own_dest[None, :] == peers[:, None]) & (own_dest[None, :] != dp_index)
    send = jnp.sum(jnp.where(leaving, own_start[None, :], 0), axis=1)
    source_base = jnp.where(senders == dp_index, grp_start, unit_count + senders) - grp_off
    covers = (
        arriving[:, :, None]
        & (units[None, None, :] >= grp_off[:, :, None])
        & (units[None, None, :] < (grp_off + grp_len)[:, :, None])
    )
    place = jnp.sum(
        jnp.where(covers, source_base[:, :, None] + units[None, None, :], 0), axis=(0, 1)
    )
    within = jnp.arange(SLOT, dtype=jnp.int32)

    def unit_rows(first):
        return (first[:, None] * SLOT + within[None, :]).reshape(-1)

    row_ids = jnp.arange(ROWS, dtype=jnp.int32)
    image = jnp.sum(jnp.where(row_ids[None, :] >= (own_start * SLOT)[:, None], 1, 0), axis=0)
    fill = (0, ROWS - dp_count * SLOT)
    columns = [
        unit_rows(home),
        unit_rows(place),
        image,
        jnp.pad(unit_rows(back), fill),
        jnp.pad(unit_rows(send), fill),
    ]
    return jnp.stack(columns, axis=1).astype(jnp.int32), image[None, :].astype(jnp.int32)


def shards(
    queries, key_vectors, value_vectors, image_lengths, image_dest, image_offset, out_weight, out_grad
):
    table, images = row_tables(image_lengths, image_dest, image_offset)
    any_space = pl.BlockSpec(memory_space=pl.ANY)
    rows = jax.ShapeDtypeStruct((ROWS, D), BF16)
    vmem = pltpu.VMEM
    dma = pltpu.SemaphoreType.DMA
    return pl.pallas_call(
        kernel,
        out_shape=(rows, rows, rows, rows, jax.ShapeDtypeStruct((SHARD, BLOCK), BF16)),
        in_specs=[pl.BlockSpec(memory_space=vmem)] * 2 + [any_space] * 5,
        out_specs=[any_space] * 5,
        scratch_shapes=[
            vmem((ROWS, D), BF16),
            vmem((ROWS, D), BF16),
            vmem((ROWS, D), BF16),
            vmem((8 * SHARD, D), BF16),
            vmem((ROWS + 8 * SLOT, D), BF16),
            vmem((8 * SLOT, D), BF16),
            vmem((8 * SLOT, D), BF16),
            vmem((2, ROWS, D), BF16),
            vmem((2, 4, ROWS, HALF), BF16),
            vmem((4, ROWS, HALF), BF16),
            vmem((4, HALF, 2 * ROWS), BF16),
            vmem((24, ROWS, ROWS), BF16),
            vmem((ROWS, ROWS), F32),
            vmem((ROWS, GROUP), BF16),
            vmem((4, ROWS, HALF), BF16),
            vmem((4, ROWS, HALF), BF16),
            vmem((4, ROWS, HALF), BF16),
            vmem((2, ROWS, BLOCK), F32),
            vmem((8, ROWS, BLOCK), BF16),
            vmem((8, ROWS, BLOCK), BF16),
            vmem((8 * SLOT, D), BF16),
            *[vmem((4, 4, 4, count, BLOCK), BF16) for _, count, _, _ in PIPES],
            *[vmem((2, 4, 4, count, BLOCK), BF16) for _, count, _, _ in PIPES],
            *[vmem((4, 4, count, BLOCK), BF16) for _, count, _, _ in PIPES],
            *[vmem((3, 4, count, BLOCK), BF16) for _, count, _, _ in PIPES],
            *[vmem((3, count, BLOCK), BF16) for _, count, _, _ in PIPES],
            vmem((SHARD, BLOCK), BF16),
            dma((5,)),
            dma((3, 4)),
            dma((3, 4)),
            dma((3, 4)),
            dma((4, 4)),
            dma((4, 4)),
            dma((2, 7)),
            dma((2, 7)),
            dma((4, 8)),
            dma((4, 8)),
            dma((4, 9)),
            dma((4, 9)),
        ],
        compiler_params=pltpu.CompilerParams(
            collective_id=0, has_side_effects=True, vmem_limit_bytes=63 * 2**20
        ),
        name="attention_step",
    )(table, images, queries, key_vectors, value_vectors, out_weight, out_grad)


def solution(mesh):
    rows = P(("dp", "fsdp"), None)
    return jax.shard_map(
        shards,
        mesh=mesh,
        in_specs=(rows, rows, rows, P(), P(), P(), P("fsdp", None), rows),
        out_specs=(rows, rows, rows, rows, P("fsdp", "dp")),
        check_vma=False,
    )
```

```python
import jax
import jax.numpy as jnp
from jax import lax
from jax.experimental import pallas as pl
from jax.experimental.pallas import tpu as pltpu
from jax.sharding import PartitionSpec as P

HD = 128
SLOT = 16
MESH = pl.DeviceIdType.MESH
F32 = jnp.float32
BF16 = jnp.bfloat16
ROWS = 288
D = 3072
GROUP = 768
HALF = 384
SHARD = 192
CHUNK = 48
BLOCK = 384
PIPES = ((0, 64, "zyx", 1), (64, 64, "zxy", 3), (128, 32, "yzx", 1), (160, 32, "yxz", 3))
SCALE = HD ** (-0.5)


def flip(index, by):
    high = lax.rem(lax.div(index, 2) + by // 2, 2)
    return high * 2 + lax.rem(lax.rem(index, 2) + by % 2, 2)


def contract(first, second, first_dim, second_dim):
    return lax.dot_general(
        first, second, (((first_dim,), (second_dim,)), ((), ())), preferred_element_type=F32
    )


def kernel(
    images,
    q_hbm,
    k_hbm,
    v_hbm,
    w_hbm,
    og_hbm,
    proj_hbm,
    dq_hbm,
    dk_hbm,
    dv_hbm,
    dw_hbm,
    qv,
    kv,
    vv,
    weight,
    pool,
    og_slots,
    slot_out,
    og_pair,
    attn_half,
    attn_out,
    attn_t,
    probs,
    bias,
    heads6,
    grad_half,
    grad_out,
    grad_in,
    part,
    part_out,
    part_in,
    proj_slots,
    term_0,
    term_1,
    term_2,
    term_3,
    pair_0,
    pair_1,
    pair_2,
    pair_3,
    quad_0,
    quad_1,
    quad_2,
    quad_3,
    next_0,
    next_1,
    next_2,
    next_3,
    last_0,
    last_1,
    last_2,
    last_3,
    dw_rows,
    table,
    load_sem,
    store_sem,
    wy_send,
    wy_recv,
    wx_send,
    wx_recv,
    a2a_send,
    a2a_recv,
    core_send,
    core_recv,
    rs_send,
    rs_recv,
):
    dp = lax.axis_index("dp")
    fs = lax.axis_index("fsdp")
    xh, z = lax.div(dp, 4), lax.rem(dp, 4)
    y, xl, core = lax.div(fs, 4), lax.rem(lax.div(fs, 2), 2), lax.rem(fs, 2)

    def device(xh_, xl_, y_, z_, core_):
        return (xh_ * 4 + z_, y_ * 4 + xl_ * 2 + core_)

    def along_x(by):
        return device(lax.rem(xh + by // 2, 2), lax.rem(xl + by % 2, 2), y, z, core)

    def along_y(by):
        return device(xh, xl, flip(y, by), z, core)

    def along_z(by):
        return device(xh, xl, y, flip(z, by), core)

    def over_dp(by):
        return device(lax.rem(xh + by // 4, 2), xl, y, flip(z, by % 4), core)

    partner = device(xh, xl, y, z, 1 - core)

    def remote(src, dst, send, recv, target):
        return pltpu.make_async_remote_copy(
            src_ref=src, dst_ref=dst, send_sem=send, recv_sem=recv, device_id=target, device_id_type=MESH
        )

    here = y * 2 + xl
    loads = [
        pltpu.make_async_copy(
            w_hbm, weight.at[pl.ds(pl.multiple_of(here * SHARD, SHARD), SHARD)], load_sem.at[0]
        ),
        pltpu.make_async_copy(og_hbm, pool.at[0:ROWS], load_sem.at[1]),
        pltpu.make_async_copy(q_hbm, qv, load_sem.at[2]),
        pltpu.make_async_copy(k_hbm, kv, load_sem.at[3]),
        pltpu.make_async_copy(v_hbm, vv, load_sem.at[4]),
    ]
    for copy in loads:
        copy.start()
    barrier = pltpu.get_barrier_semaphore()
    peers = (
        [along_x(by) for by in (1, 2, 3)]
        + [along_y(by) for by in (1, 2, 3)]
        + [along_z(by) for by in (1, 2, 3)]
        + [over_dp(by) for by in (5, 6, 7)]
        + [partner]
    )
    for peer in peers:
        pl.semaphore_signal(barrier, inc=1, device_id=peer, device_id_type=MESH)

    width = images.shape[1] // 3

    def images_of(dp_):
        rows = pl.ds(dp_ * 16 + fs, 1)
        length, dest, offset = (images[rows, i * width : (i + 1) * width] for i in range(3))
        lane = lax.broadcasted_iota(jnp.int32, length.shape, 1)
        start = jnp.zeros_like(length)
        for image in range(length.shape[1] - 1):
            start += jnp.where(lane > image, length[:, image : image + 1], 0)
        return length, dest, offset, start

    def sum_lanes(hit, value):
        return jnp.sum(jnp.where(hit, value, 0), axis=1, keepdims=True)

    length, dest, offset, start = images_of(dp)
    row = lax.broadcasted_iota(jnp.int32, (ROWS, 1), 0)
    inside = (row >= start) & (row < start + length)
    table[:, 0:1] = sum_lanes(
        inside, jnp.where(dest == dp, offset, ROWS + SLOT * dest) - start + row
    )
    slot_row = lax.broadcasted_iota(jnp.int32, (8 * SLOT, 1), 0)
    slot, in_slot = lax.div(slot_row, SLOT), lax.rem(slot_row, SLOT)
    table[: 8 * SLOT, 3:4] = (
        sum_lanes((dest == slot) & (dest != dp), start + in_slot + 1) - 1
    )
    columns = lax.broadcasted_iota(jnp.int32, (1, ROWS), 1)
    row_image = jnp.zeros((ROWS, 1), jnp.int32)
    column_image = jnp.zeros((1, ROWS), jnp.int32)
    for image in range(1, length.shape[1]):
        first = start[:, image : image + 1]
        row_image += jnp.where(row >= first, 1, 0)
        column_image += jnp.where(columns >= first, 1, 0)
    bias[...] = jnp.where(row_image == column_image, 0.0, -1e30).astype(F32)

    senders = [images_of(sender) for sender in range(8)]
    length, dest, offset, start = [jnp.concatenate(list(part), axis=1) for part in zip(*senders)]
    sender = lax.div(lax.broadcasted_iota(jnp.int32, length.shape, 1), width)
    covers = (dest == dp) & (row >= offset) & (row < offset + length)
    table[:, 1:2] = sum_lanes(
        covers, jnp.where(sender == dp, start, ROWS + SLOT * sender) - offset + row
    )
    table[: 8 * SLOT, 2:3] = (
        sum_lanes((sender == slot) & (dest == dp) & (sender != dp), offset + in_slot + 1) - 1
    )

    def pick(column, out_rows, in_rows, dst, dst_core=None):
        chosen = lax.broadcasted_iota(jnp.int32, (out_rows, in_rows), 1) == (
            table[:out_rows, column : column + 1]
        )
        one_hot = jnp.where(chosen, 1.0, 0.0).astype(BF16)

        def one_part(i, carry):
            cols = pl.ds(pl.multiple_of(i * GROUP, GROUP), GROUP)
            rows = contract(one_hot, pool[:in_rows, cols], 1, 0).astype(BF16)
            if dst_core is None:
                dst[:, cols] = rows
            else:
                dst[dst_core, :, cols] = rows
            return carry

        lax.fori_loop(0, D // GROUP, one_part, 0)

    pl.semaphore_wait(barrier, len(peers))

    def shard_rows(y_, xl_, chunk):
        return pl.ds(pl.multiple_of((y_ * 2 + xl_) * SHARD + chunk * CHUNK, CHUNK), CHUNK)

    def w_along_y(by, chunk):
        via = (1 if chunk < 2 else 3) if by == 2 else 0
        rows = weight.at[shard_rows(flip(y, via), xl, chunk)]
        return remote(
            rows,
            rows,
            wy_send.at[by - 1, chunk],
            wy_recv.at[by - 1, chunk],
            along_y(4 - via if by == 2 else by),
        )

    def w_along_x(by, chunk):
        rows = weight.at[shard_rows(flip(y, by), xl, chunk)]
        return remote(
            rows,
            rows,
            wx_send.at[by, chunk],
            wx_recv.at[by, chunk],
            along_x(1 if chunk % 2 == 0 else 3),
        )

    def forward(by, chunk):
        w_along_y(by, chunk).wait_recv()
        if by == (1 if chunk < 2 else 3):
            w_along_y(2, chunk).start()
        w_along_x(by, chunk).start()

    loads[0].wait()
    for step in range(4):
        w_along_y(1, step).start()
        w_along_y(3, 3 - step).start()
        w_along_x(0, step).start()

    def unit(index):
        return pl.ds(pl.multiple_of(index * SLOT, SLOT), SLOT)

    def slots(by, dst, phase):
        to_dp = lax.rem(xh + by // 4, 2) * 4 + flip(z, by % 4)
        return remote(
            slot_out.at[unit(to_dp)],
            dst.at[unit(dp)],
            a2a_send.at[phase, by - 1],
            a2a_recv.at[phase, by - 1],
            over_dp(by),
        )

    loads[1].wait()
    pick(2, 8 * SLOT, ROWS, slot_out)
    own_slot = jnp.zeros((SLOT, D), BF16)
    og_slots[unit(dp), :] = own_slot
    proj_slots[unit(dp), :] = own_slot
    for by in range(1, 8):
        slots(by, og_slots, 0).start()
    for copy in loads[2:]:
        copy.wait()

    def head_cols(head):
        return pl.ds(pl.multiple_of(head * HD, HD), HD)

    def split_cores(first, second):
        mine = jnp.where(core == 0, first, second)
        other = jnp.where(core == 0, second, first)
        return mine, other

    def attn_copy(group):
        return remote(
            attn_out.at[group],
            attn_half.at[core, group],
            core_send.at[0, group],
            core_recv.at[0, group],
            partner,
        )

    def attend(group):
        def one_head(i, carry):
            head = group * 6 + i
            cols = head_cols(head)
            scores = contract(qv[:, cols], kv[:, cols], 1, 1) * SCALE + bias[...]
            powers = jnp.exp(scores - jnp.max(scores, axis=1, keepdims=True))
            inverse = 1.0 / jnp.sum(powers, axis=1, keepdims=True)
            weights = (powers * inverse).astype(BF16)
            probs[head] = weights
            heads6[:, head_cols(i)] = contract(weights, vv[:, cols], 1, 0).astype(BF16)
            return carry

        lax.fori_loop(0, 6, one_head, 0)
        for t in range(2):
            first = heads6[:, t * HALF : t * HALF + SHARD]
            second = heads6[:, t * HALF + SHARD : (t + 1) * HALF]
            mine, other = split_cores(first, second)
            attn_half[core, group, :, t * SHARD : (t + 1) * SHARD] = mine
            attn_out[group, :, t * SHARD : (t + 1) * SHARD] = other
        attn_copy(group).start()

    attend(0)
    attend(1)
    forward(1, 0)
    forward(3, 3)
    attend(2)

    for by in range(1, 8):
        slots(by, og_slots, 0).wait_recv()
    pool[ROWS:, :] = og_slots[...]
    pick(0, ROWS, ROWS + 8 * SLOT, og_pair, core)
    og_copy = remote(
        og_pair.at[core], og_pair.at[core], core_send.at[1, 0], core_recv.at[1, 0], partner
    )
    og_copy.start()
    attend(3)
    forward(1, 1)
    forward(3, 2)

    for group in range(4):
        attn_copy(group).wait_recv()
        attn_t[group] = attn_half[:, group].reshape(2 * ROWS, HALF).T
    og_copy.wait_recv()

    grad_scale = (ROWS * 128) ** (-0.5)

    x = xh * 2 + xl
    here_on = {"x": x, "y": y, "z": z}
    along = {"x": along_x, "y": along_y, "z": along_z}
    terms = (term_0, term_1, term_2, term_3)
    pairs = (pair_0, pair_1, pair_2, pair_3)
    quads = (quad_0, quad_1, quad_2, quad_3)
    nexts = (next_0, next_1, next_2, next_3)
    lasts = (last_0, last_1, last_2, last_3)

    def first_copy(pipe, by, z_):
        near = PIPES[pipe][3]
        slot = 0 if by == 2 else 1
        term, pair = terms[pipe], pairs[pipe].at[slot]
        if pipe < 2:
            src, dst = term.at[z_], pair
        elif pipe == 2:
            src, dst = term.at[flip(y, by), z_], pair.at[z_]
        else:
            src, dst = term.at[flip(y, by), :, z_], pair.at[:, z_]
        return remote(
            src, dst, rs_send.at[pipe, slot], rs_recv.at[pipe, slot], along[PIPES[pipe][2][0]](near)
        )

    def compute_terms(by_z):
        z_ = flip(z, by_z)

        def one_term(by_xh, carry):
            xh_ = lax.rem(xh + 1 + by_xh, 2)
            cols = pl.ds(pl.multiple_of((xh_ * 4 + z_) * BLOCK, BLOCK), BLOCK)
            grads = og_pair[:, :, cols].reshape(2 * ROWS, BLOCK)
            for y_ in range(4):
                term = (contract(attn_t[y_], grads, 1, 0) * grad_scale).astype(BF16)
                for xl_ in range(2):
                    x_ = xh_ * 2 + xl_
                    places = ((z_, y_, x_), (z_, x_, y_), (y_, z_, x_), (y_, x_, z_))
                    for (first_row, count, _, _), buffer, place in zip(PIPES, terms, places):
                        at = xl_ * SHARD + first_row
                        buffer[place] = term[at : at + count]
            return carry

        lax.fori_loop(0, 2, one_term, 0)
        for pipe in range(4):
            near = PIPES[pipe][3]
            if pipe < 2:
                if by_z in (2, near):
                    first_copy(pipe, by_z, z_).start()
            else:
                first_copy(pipe, 2, z_).start()
                first_copy(pipe, near, z_).start()

    compute_terms(2)
    forward(1, 2)
    forward(3, 1)
    compute_terms(1)
    compute_terms(3)
    forward(1, 3)
    forward(3, 0)
    compute_terms(0)

    def grad_copy(by):
        return remote(
            grad_out.at[by], grad_in.at[by], core_send.at[2, by], core_recv.at[2, by], partner
        )

    def attn_grad(by):
        for chunk in range(4):
            w_along_x(by, chunk).wait_recv()
        rows = pl.ds(pl.multiple_of(flip(y, by) * HALF, HALF), HALF)

        def one_side(side, carry):
            owner = lax.rem(1 - core + side, 2)
            half = contract(og_pair[owner], weight[rows, :], 1, 1).astype(BF16)

            @pl.when(side == 0)
            def _():
                grad_out[by] = half

            @pl.when(side == 1)
            def _():
                grad_half[by] = half

            return carry

        one_side(0, 0)
        grad_copy(by).start()
        one_side(1, 0)

    def store_copy(by, which):
        cols = pl.ds(pl.multiple_of(flip(y, by) * GROUP, GROUP), GROUP)
        src = (qv, kv, vv)[which]
        dst = (dq_hbm, dk_hbm, dv_hbm)[which]
        return pltpu.make_async_copy(src.at[:, cols], dst.at[:, cols], store_sem.at[which, by])

    def attend_back(by):
        grad_copy(by).wait_recv()
        for t in range(2):
            mine = grad_half[by, :, t * SHARD : (t + 1) * SHARD]
            other = grad_in[by, :, t * SHARD : (t + 1) * SHARD]
            first, second = split_cores(mine, other)
            heads6[:, t * HALF : t * HALF + SHARD] = first
            heads6[:, t * HALF + SHARD : (t + 1) * HALF] = second

        def one_head(i, carry):
            head = flip(y, by) * 6 + i
            cols = head_cols(head)
            grads = heads6[:, head_cols(i)]
            weights = probs[head]
            wide = weights.astype(F32)
            queries, keys = qv[:, cols], kv[:, cols]
            products = contract(grads, vv[:, cols], 1, 1) * wide
            total = jnp.sum(products, axis=1, keepdims=True)
            score_grad = ((products - wide * total) * SCALE).astype(BF16)
            vv[:, cols] = contract(weights, grads, 0, 0).astype(BF16)
            qv[:, cols] = contract(score_grad, keys, 1, 0).astype(BF16)
            kv[:, cols] = contract(score_grad, queries, 0, 0).astype(BF16)
            return carry

        lax.fori_loop(0, 6, one_head, 0)
        for which in range(3):
            store_copy(by, which).start()

    def all_of(buffer, sem):
        return pltpu.make_async_copy(buffer, buffer, sem)

    def summed(own, others):
        total = own.astype(F32)
        for other in others:
            total += other.astype(F32)
        return total.astype(BF16)

    def second_copy(pipe, half):
        _, _, axes, near = PIPES[pipe]
        rows = pl.ds(half * 2, 2)
        return remote(
            terms[pipe].at[flip(here_on[axes[0]], 4 - near), rows],
            quads[pipe].at[rows],
            rs_send.at[pipe, 2],
            rs_recv.at[pipe, 2],
            along[axes[0]](4 - near),
        )

    def pipe_second(pipe):
        term, pair = terms[pipe], pairs[pipe]
        far = flip(here_on[PIPES[pipe][2][0]], 4 - PIPES[pipe][3])
        all_of(pair.at[0], rs_recv.at[pipe, 0]).wait()
        for half in range(2):

            def one_block(i, carry):
                second, third = half * 2 + lax.div(i, 4), lax.rem(i, 4)
                term[far, second, third] = summed(
                    term[far, second, third], [pair[0, second, third]]
                )
                return carry

            lax.fori_loop(0, 8, one_block, 0)
            second_copy(pipe, half).start()

    def third_copy(pipe, by):
        axes = PIPES[pipe][2]
        return remote(
            terms[pipe].at[here_on[axes[0]], flip(here_on[axes[1]], by)],
            nexts[pipe].at[by - 1],
            rs_send.at[pipe, 2 + by],
            rs_recv.at[pipe, 2 + by],
            along[axes[1]](by),
        )

    def pipe_third(pipe):
        term, pair, quad = terms[pipe], pairs[pipe], quads[pipe]
        own = here_on[PIPES[pipe][2][0]]
        all_of(pair.at[1], rs_recv.at[pipe, 1]).wait()
        all_of(quad, rs_recv.at[pipe, 2]).wait()

        def one_block(i, carry):
            second, third = lax.div(i, 4), lax.rem(i, 4)
            term[own, second, third] = summed(
                term[own, second, third], [pair[1, second, third], quad[second, third]]
            )
            return carry

        lax.fori_loop(0, 16, one_block, 0)
        for by in (2, 1, 3):
            third_copy(pipe, by).start()

    def fourth_copy(pipe, by):
        axes = PIPES[pipe][2]
        return remote(
            terms[pipe].at[here_on[axes[0]], here_on[axes[1]], flip(here_on[axes[2]], by)],
            lasts[pipe].at[by - 1],
            rs_send.at[pipe, 5 + by],
            rs_recv.at[pipe, 5 + by],
            along[axes[2]](by),
        )

    def pipe_fourth(pipe):
        term, arrived = terms[pipe], nexts[pipe]
        axes = PIPES[pipe][2]
        own = here_on[axes[0]], here_on[axes[1]]
        for by in (1, 2, 3):
            third_copy(pipe, by).wait_recv()

        def one_block(third, carry):
            place = own + (third,)
            term[place] = summed(term[place], [arrived[r, third] for r in range(3)])
            return carry

        lax.fori_loop(0, 4, one_block, 0)
        for by in (2, 1, 3):
            fourth_copy(pipe, by).start()

    def pipe_last(pipe):
        first_row, count, axes, _ = PIPES[pipe]
        for by in (1, 2, 3):
            fourth_copy(pipe, by).wait_recv()
        dw_rows[first_row : first_row + count, :] = summed(
            terms[pipe][tuple(here_on[axis] for axis in axes)], [lasts[pipe][r] for r in range(3)]
        )

    attn_grad(0)
    attend_back(0)
    forward(2, 0)
    forward(2, 3)
    attn_grad(1)
    attend_back(1)
    forward(2, 1)
    forward(2, 2)
    pipe_second(0)
    pipe_second(1)
    attn_grad(3)
    attend_back(3)
    pipe_second(2)
    pipe_second(3)
    attn_grad(2)

    def part_copy(block):
        return remote(
            part_out.at[block], part_in.at[block], core_send.at[3, block], core_recv.at[3, block],
            partner,
        )

    def one_block(block, carry):
        cols = pl.ds(pl.multiple_of(block * BLOCK, BLOCK), BLOCK)
        total = jnp.zeros((2 * ROWS, BLOCK), F32)
        for group in range(4):
            total += contract(
                attn_half[:, group].reshape(2 * ROWS, HALF),
                weight[group * HALF : (group + 1) * HALF, cols],
                1,
                0,
            )
        part[...] = total.reshape(2, ROWS, BLOCK)
        part_out[block] = part[1 - core].astype(BF16)
        part_copy(block).start()
        pool[:ROWS, cols] = part[core].astype(BF16)
        return carry

    lax.fori_loop(0, 8, one_block, 0)

    def add_block(block, carry):
        cols = pl.ds(pl.multiple_of(block * BLOCK, BLOCK), BLOCK)
        part_copy(block).wait_recv()
        pool[:ROWS, cols] = (
            pool[:ROWS, cols].astype(F32) + part_in[block].astype(F32)
        ).astype(BF16)
        return carry

    lax.fori_loop(0, 8, add_block, 0)

    for by in range(1, 8):
        slots(by, og_slots, 0).wait_send()
    pick(3, 8 * SLOT, ROWS, slot_out)
    for by in range(1, 8):
        slots(by, proj_slots, 1).start()

    attend_back(2)

    for pipe in (2, 3, 0, 1):
        pipe_third(pipe)

    for by in range(1, 8):
        slots(by, proj_slots, 1).wait_recv()
    pool[ROWS:, :] = proj_slots[...]
    og_copy.wait_send()
    pick(1, ROWS, ROWS + 8 * SLOT, og_pair, core)
    proj_copy = pltpu.make_async_copy(og_pair.at[core], proj_hbm, load_sem.at[0])
    proj_copy.start()

    for pipe in (2, 3, 0, 1):
        pipe_fourth(pipe)
    for pipe in (2, 3, 0, 1):
        pipe_last(pipe)
    dw_copy = pltpu.make_async_copy(dw_rows, dw_hbm, load_sem.at[1])
    dw_copy.start()

    for by in range(4):
        for chunk in range(4):
            if by > 0:
                w_along_y(by, chunk).wait_send()
            w_along_x(by, chunk).wait_send()
        attn_copy(by).wait_send()
        grad_copy(by).wait_send()
    for by in range(1, 8):
        slots(by, proj_slots, 1).wait_send()
    for block in range(8):
        part_copy(block).wait_send()
    for pipe in range(4):
        for slot in range(2):
            all_of(pairs[pipe].at[slot], rs_send.at[pipe, slot]).wait()
        all_of(quads[pipe], rs_send.at[pipe, 2]).wait()
        for by in (1, 2, 3):
            third_copy(pipe, by).wait_send()
            fourth_copy(pipe, by).wait_send()
    for by in range(4):
        for which in range(3):
            store_copy(by, which).wait()
    proj_copy.wait()
    dw_copy.wait()


def store_kernel(*refs):
    count = len(refs) // 3
    sources, targets, buffers = refs[:count], refs[count : 2 * count], refs[2 * count : 3 * count]
    load_sem, store_sem = refs[-2:]
    loads, stores = [], []
    for i, (src, dst, held) in enumerate(zip(sources, targets, buffers)):
        rows = src.shape[0] // 3
        for part in range(3):
            at = pl.ds(part * rows, rows)
            loads.append(pltpu.make_async_copy(src.at[at], held.at[at], load_sem.at[i, part]))
            stores.append(pltpu.make_async_copy(held.at[at], dst.at[at], store_sem.at[i, part]))
    for copy in loads:
        copy.start()
    for arrived, copy in zip(loads, stores):
        arrived.wait()
        copy.start()
    for copy in stores:
        copy.wait()


def store(results):
    any_space = pl.BlockSpec(memory_space=pl.ANY)
    return pl.pallas_call(
        store_kernel,
        out_shape=[jax.ShapeDtypeStruct(result.shape, result.dtype) for result in results],
        in_specs=[any_space] * len(results),
        out_specs=[any_space] * len(results),
        scratch_shapes=[pltpu.VMEM(result.shape, result.dtype) for result in results]
        + [pltpu.SemaphoreType.DMA((len(results), 3))] * 2,
        compiler_params=pltpu.CompilerParams(vmem_limit_bytes=63 * 2**20),
        name="store_results",
    )(*results)


def shards(
    queries, key_vectors, value_vectors, image_lengths, image_dest, image_offset, out_weight, out_grad
):
    any_space = pl.BlockSpec(memory_space=pl.ANY)
    rows = jax.ShapeDtypeStruct((ROWS, D), BF16)
    vmem = pltpu.VMEM
    dma = pltpu.SemaphoreType.DMA
    results = pl.pallas_call(
        kernel,
        out_shape=(rows, rows, rows, rows, jax.ShapeDtypeStruct((SHARD, BLOCK), BF16)),
        in_specs=[pl.BlockSpec(memory_space=vmem)] + [any_space] * 5,
        out_specs=[any_space] * 5,
        scratch_shapes=[
            vmem((ROWS, D), BF16),
            vmem((ROWS, D), BF16),
            vmem((ROWS, D), BF16),
            vmem((8 * SHARD, D), BF16),
            vmem((ROWS + 8 * SLOT, D), BF16),
            vmem((8 * SLOT, D), BF16),
            vmem((8 * SLOT, D), BF16),
            vmem((2, ROWS, D), BF16),
            vmem((2, 4, ROWS, HALF), BF16),
            vmem((4, ROWS, HALF), BF16),
            vmem((4, HALF, 2 * ROWS), BF16),
            vmem((24, ROWS, ROWS), BF16),
            vmem((ROWS, ROWS), F32),
            vmem((ROWS, GROUP), BF16),
            vmem((4, ROWS, HALF), BF16),
            vmem((4, ROWS, HALF), BF16),
            vmem((4, ROWS, HALF), BF16),
            vmem((2, ROWS, BLOCK), F32),
            vmem((8, ROWS, BLOCK), BF16),
            vmem((8, ROWS, BLOCK), BF16),
            vmem((8 * SLOT, D), BF16),
            *[vmem((4, 4, 4, count, BLOCK), BF16) for _, count, _, _ in PIPES],
            *[vmem((2, 4, 4, count, BLOCK), BF16) for _, count, _, _ in PIPES],
            *[vmem((4, 4, count, BLOCK), BF16) for _, count, _, _ in PIPES],
            *[vmem((3, 4, count, BLOCK), BF16) for _, count, _, _ in PIPES],
            *[vmem((3, count, BLOCK), BF16) for _, count, _, _ in PIPES],
            vmem((SHARD, BLOCK), BF16),
            vmem((ROWS, HD), jnp.int32),
            dma((5,)),
            dma((3, 4)),
            dma((3, 4)),
            dma((3, 4)),
            dma((4, 4)),
            dma((4, 4)),
            dma((2, 7)),
            dma((2, 7)),
            dma((4, 8)),
            dma((4, 8)),
            dma((4, 9)),
            dma((4, 9)),
        ],
        compiler_params=pltpu.CompilerParams(
            collective_id=0, has_side_effects=True, vmem_limit_bytes=63 * 2**20
        ),
        name="attention_step",
    )(
        jnp.concatenate([image_lengths, image_dest, image_offset], axis=1),
        queries,
        key_vectors,
        value_vectors,
        out_weight,
        out_grad,
    )
    return tuple(store(results))


def solution(mesh):
    rows = P(("dp", "fsdp"), None)
    return jax.shard_map(
        shards,
        mesh=mesh,
        in_specs=(rows, rows, rows, P(), P(), P(), P("fsdp", None), rows),
        out_specs=(rows, rows, rows, rows, P("fsdp", "dp")),
        check_vma=False,
    )
```

```python
import jax
import jax.numpy as jnp
from jax import lax
from jax.experimental import pallas as pl
from jax.experimental.pallas import tpu as pltpu
from jax.sharding import PartitionSpec as P

HD = 128
SLOT = 16
MESH = pl.DeviceIdType.MESH
F32 = jnp.float32
BF16 = jnp.bfloat16
ROWS = 288
D = 3072
GROUP = 768
HALF = 384
SHARD = 192
CHUNK = 48
BLOCK = 384
PIPES = ((0, 64, "zyx", 1), (64, 48, "zxy", 3), (112, 48, "yzx", 1), (160, 32, "yxz", 3))
SCALE = HD ** (-0.5)
TOGETHER = 2
WIDE = 512


def flip(index, by):
    high = lax.rem(lax.div(index, 2) + by // 2, 2)
    return high * 2 + lax.rem(lax.rem(index, 2) + by % 2, 2)


def contract(first, second, first_dim, second_dim):
    return lax.dot_general(
        first, second, (((first_dim,), (second_dim,)), ((), ())), preferred_element_type=F32
    )


def kernel(
    images,
    q_hbm,
    k_hbm,
    v_hbm,
    w_hbm,
    og_hbm,
    proj_hbm,
    dq_hbm,
    dk_hbm,
    dv_hbm,
    dw_hbm,
    qv,
    kv,
    vv,
    weight,
    pool,
    og_slots,
    slot_out,
    og_pair,
    attn_half,
    attn_out,
    attn_t,
    probs,
    bias,
    heads6,
    grad_half,
    grad_out,
    grad_in,
    part,
    part_out,
    part_in,
    proj_slots,
    term_0,
    term_1,
    term_2,
    term_3,
    pair_0,
    pair_1,
    pair_2,
    pair_3,
    quad_0,
    quad_1,
    quad_2,
    quad_3,
    next_0,
    next_1,
    next_2,
    next_3,
    last_0,
    last_1,
    last_2,
    last_3,
    dw_rows,
    table,
    load_sem,
    store_sem,
    wy_send,
    wy_recv,
    wx_send,
    wx_recv,
    a2a_send,
    a2a_recv,
    core_send,
    core_recv,
    rs_send,
    rs_recv,
):
    dp = lax.axis_index("dp")
    fs = lax.axis_index("fsdp")
    xh, z = lax.div(dp, 4), lax.rem(dp, 4)
    y, xl, core = lax.div(fs, 4), lax.rem(lax.div(fs, 2), 2), lax.rem(fs, 2)

    def device(xh_, xl_, y_, z_, core_):
        return (xh_ * 4 + z_, y_ * 4 + xl_ * 2 + core_)

    def along_x(by):
        return device(lax.rem(xh + by // 2, 2), lax.rem(xl + by % 2, 2), y, z, core)

    def along_y(by):
        return device(xh, xl, flip(y, by), z, core)

    def along_z(by):
        return device(xh, xl, y, flip(z, by), core)

    def over_dp(by):
        return device(lax.rem(xh + by // 4, 2), xl, y, flip(z, by % 4), core)

    partner = device(xh, xl, y, z, 1 - core)

    def remote(src, dst, send, recv, target):
        return pltpu.make_async_remote_copy(
            src_ref=src, dst_ref=dst, send_sem=send, recv_sem=recv, device_id=target, device_id_type=MESH
        )

    here = y * 2 + xl
    loads = [
        pltpu.make_async_copy(
            w_hbm, weight.at[pl.ds(pl.multiple_of(here * SHARD, SHARD), SHARD)], load_sem.at[0]
        ),
        pltpu.make_async_copy(og_hbm, pool.at[0:ROWS], load_sem.at[1]),
        pltpu.make_async_copy(q_hbm, qv, load_sem.at[2]),
        pltpu.make_async_copy(k_hbm, kv, load_sem.at[3]),
        pltpu.make_async_copy(v_hbm, vv, load_sem.at[4]),
    ]
    for copy in loads:
        copy.start()
    barrier = pltpu.get_barrier_semaphore()
    peers = (
        [along_x(by) for by in (1, 2, 3)]
        + [along_y(by) for by in (1, 2, 3)]
        + [along_z(by) for by in (1, 2, 3)]
        + [over_dp(by) for by in (5, 6, 7)]
        + [partner]
    )
    for peer in peers:
        pl.semaphore_signal(barrier, inc=1, device_id=peer, device_id_type=MESH)

    width = images.shape[1] // 3

    def images_of(dp_):
        rows = pl.ds(dp_ * 16 + fs, 1)
        length, dest, offset = (images[rows, i * width : (i + 1) * width] for i in range(3))
        lane = lax.broadcasted_iota(jnp.int32, length.shape, 1)
        start = jnp.zeros_like(length)
        for image in range(length.shape[1] - 1):
            start += jnp.where(lane > image, length[:, image : image + 1], 0)
        return length, dest, offset, start

    def sum_lanes(hit, value):
        return jnp.sum(jnp.where(hit, value, 0), axis=1, keepdims=True)

    row = lax.broadcasted_iota(jnp.int32, (ROWS, 1), 0)
    senders = [images_of(sender) for sender in range(8)]
    first_rows = lax.broadcasted_iota(jnp.int32, (SLOT, 1), 0) + 1
    for sender, (_, dest, offset, _) in enumerate(senders):
        arrives = (dest == dp) & (dp != sender)
        table[sender * SLOT : (sender + 1) * SLOT, 2:3] = (
            sum_lanes(arrives, offset + first_rows) - 1
        )

    pl.semaphore_wait(barrier, len(peers))

    def shard_rows(y_, xl_, chunk):
        return pl.ds(pl.multiple_of((y_ * 2 + xl_) * SHARD + chunk * CHUNK, CHUNK), CHUNK)

    def w_along_y(by, chunk):
        via = (1 if chunk < 2 else 3) if by == 2 else 0
        rows = weight.at[shard_rows(flip(y, via), xl, chunk)]
        return remote(
            rows,
            rows,
            wy_send.at[by - 1, chunk],
            wy_recv.at[by - 1, chunk],
            along_y(4 - via if by == 2 else by),
        )

    def w_along_x(by, chunk):
        rows = weight.at[shard_rows(flip(y, by), xl, chunk)]
        return remote(
            rows,
            rows,
            wx_send.at[by, chunk],
            wx_recv.at[by, chunk],
            along_x(1 if chunk % 2 == 0 else 3),
        )

    def forward(by, chunk):
        w_along_y(by, chunk).wait_recv()
        if by == (1 if chunk < 2 else 3):
            w_along_y(2, chunk).start()
        w_along_x(by, chunk).start()

    loads[0].wait()
    for step in range(4):
        w_along_y(1, step).start()
        w_along_y(3, 3 - step).start()
    w_along_x(0, 0).start()
    w_along_x(0, 3).start()

    def pick(column, out_rows, in_rows, dst, dst_core=None):
        chosen = lax.broadcasted_iota(jnp.int32, (out_rows, in_rows), 1) == (
            table[:out_rows, column : column + 1]
        )
        one_hot = jnp.where(chosen, 1.0, 0.0).astype(BF16)

        def one_part(i, carry):
            cols = pl.ds(pl.multiple_of(i * GROUP, GROUP), GROUP)
            rows = contract(one_hot, pool[:in_rows, cols], 1, 0).astype(BF16)
            if dst_core is None:
                dst[:, cols] = rows
            else:
                dst[dst_core, :, cols] = rows
            return carry

        lax.fori_loop(0, D // GROUP, one_part, 0)

    def unit(index):
        return pl.ds(pl.multiple_of(index * SLOT, SLOT), SLOT)

    def slots(by, dst, phase):
        to_dp = lax.rem(xh + by // 4, 2) * 4 + flip(z, by % 4)
        return remote(
            slot_out.at[unit(to_dp)],
            dst.at[unit(dp)],
            a2a_send.at[phase, by - 1],
            a2a_recv.at[phase, by - 1],
            over_dp(by),
        )

    loads[1].wait()
    pick(2, 8 * SLOT, ROWS, slot_out)
    own_slot = jnp.zeros((SLOT, D), BF16)
    og_slots[unit(dp), :] = own_slot
    proj_slots[unit(dp), :] = own_slot
    for by in range(1, 8):
        slots(by, og_slots, 0).start()
    w_along_x(0, 1).start()
    w_along_x(0, 2).start()
    length, dest, offset, start = [jnp.concatenate(list(part), axis=1) for part in zip(*senders)]
    sender = lax.div(lax.broadcasted_iota(jnp.int32, length.shape, 1), width)
    covers = (dest == dp) & (row >= offset) & (row < offset + length)
    table[:, 1:2] = sum_lanes(
        covers, jnp.where(sender == dp, start, ROWS + SLOT * sender) - offset + row
    )
    own_length, own_dest, own_offset, own_start = images_of(dp)
    slot_row = lax.broadcasted_iota(jnp.int32, (8 * SLOT, 1), 0)
    slot, in_slot = lax.div(slot_row, SLOT), lax.rem(slot_row, SLOT)
    inside = (row >= own_start) & (row < own_start + own_length)
    table[:, 0:1] = sum_lanes(
        inside, jnp.where(own_dest == dp, own_offset, ROWS + SLOT * own_dest) - own_start + row
    )
    table[: 8 * SLOT, 3:4] = (
        sum_lanes((own_dest == slot) & (own_dest != dp), own_start + in_slot + 1) - 1
    )
    columns = lax.broadcasted_iota(jnp.int32, (1, ROWS), 1)
    row_image = jnp.zeros((ROWS, 1), jnp.int32)
    column_image = jnp.zeros((1, ROWS), jnp.int32)
    for image in range(1, width):
        first = own_start[:, image : image + 1]
        row_image += jnp.where(row >= first, 1, 0)
        column_image += jnp.where(columns >= first, 1, 0)
    bias[...] = jnp.where(row_image == column_image, 0.0, -1e30).astype(F32)

    for copy in loads[2:]:
        copy.wait()

    def head_cols(head):
        return pl.ds(pl.multiple_of(head * HD, HD), HD)

    def split_cores(first, second):
        mine = jnp.where(core == 0, first, second)
        other = jnp.where(core == 0, second, first)
        return mine, other

    def attn_copy(by):
        group = flip(y, by)
        return remote(
            attn_out.at[group],
            attn_half.at[core, group],
            core_send.at[0, by],
            core_recv.at[0, by],
            partner,
        )

    def attend(by):
        group = flip(y, by)

        def some_heads(i, carry):
            at = [i * TOGETHER + t for t in range(TOGETHER)]
            cols = [head_cols(group * 6 + n) for n in at]
            loaded = [(qv[:, c], kv[:, c], vv[:, c]) for c in cols]
            scores = [contract(q, k, 1, 1) * SCALE + bias[...] for q, k, _ in loaded]
            powers = [jnp.exp(score - jnp.max(score, axis=1, keepdims=True)) for score in scores]
            weights = [
                (power * (1.0 / jnp.sum(power, axis=1, keepdims=True))).astype(BF16)
                for power in powers
            ]
            mixed = [contract(w, v, 1, 0).astype(BF16) for w, (_, _, v) in zip(weights, loaded)]
            for n, w, attn in zip(at, weights, mixed):
                probs[group * 6 + n] = w
                heads6[:, head_cols(n)] = attn
            return carry

        lax.fori_loop(0, 6 // TOGETHER, some_heads, 0)
        for t in range(2):
            first = heads6[:, t * HALF : t * HALF + SHARD]
            second = heads6[:, t * HALF + SHARD : (t + 1) * HALF]
            mine, other = split_cores(first, second)
            attn_half[core, group, :, t * SHARD : (t + 1) * SHARD] = mine
            attn_out[group, :, t * SHARD : (t + 1) * SHARD] = other
        attn_copy(by).start()

    attend(2)
    attend(1)
    forward(1, 0)
    forward(3, 3)

    for by in range(1, 8):
        slots(by, og_slots, 0).wait_recv()
    pool[ROWS:, :] = og_slots[...]
    pick(0, ROWS, ROWS + 8 * SLOT, og_pair, core)
    og_copy = remote(
        og_pair.at[core], og_pair.at[core], core_send.at[1, 0], core_recv.at[1, 0], partner
    )
    og_copy.start()
    attend(3)
    forward(1, 1)
    forward(3, 2)
    og_copy.wait_recv()

    grad_scale = (ROWS * 128) ** (-0.5)

    x = xh * 2 + xl
    here_on = {"x": x, "y": y, "z": z}
    along = {"x": along_x, "y": along_y, "z": along_z}
    terms = (term_0, term_1, term_2, term_3)
    pairs = (pair_0, pair_1, pair_2, pair_3)
    quads = (quad_0, quad_1, quad_2, quad_3)
    nexts = (next_0, next_1, next_2, next_3)
    lasts = (last_0, last_1, last_2, last_3)

    def first_copy(pipe, slot, by):
        _, _, axes, near = PIPES[pipe]
        toward = flip(here_on[axes[0]], 2 if slot == 0 else near)
        term, pair, group = terms[pipe], pairs[pipe], flip(y, by)
        if pipe == 0:
            src, dst = term.at[toward, group], pair.at[slot, group]
        elif pipe == 1:
            src, dst = term.at[toward, :, group], pair.at[slot, :, group]
        else:
            src, dst = term.at[toward], pair.at[slot]
        sem = slot * 4 + by
        return remote(src, dst, rs_send.at[pipe, sem], rs_recv.at[pipe, sem], along[axes[0]](near))

    def compute_terms(by):
        group = flip(y, by)
        attn_copy(by).wait_recv()
        attn_t[...] = attn_half[:, group].reshape(2 * ROWS, HALF).T
        for by_z in (2, 1, 3, 0):
            z_ = flip(z, by_z)

            columns_of = [
                pl.ds(pl.multiple_of((xh_ * 4 + z_) * BLOCK, BLOCK), BLOCK) for xh_ in range(2)
            ]
            grads = jnp.concatenate(
                [og_pair[:, :, cols].reshape(2 * ROWS, BLOCK) for cols in columns_of], axis=1
            )
            term = (contract(attn_t[...], grads, 1, 0) * grad_scale).astype(BF16)
            for x_ in range(4):
                places = ((z_, group, x_), (z_, x_, group), (group, z_, x_), (group, x_, z_))
                left = (x_ // 2) * BLOCK
                for (first_row, count, _, _), buffer, place in zip(PIPES, terms, places):
                    at = (x_ % 2) * SHARD + first_row
                    buffer[place] = term[at : at + count, left : left + BLOCK]
            for pipe in range(2):
                if by_z in (2, PIPES[pipe][3]):
                    first_copy(pipe, 0 if by_z == 2 else 1, by).start()
        for pipe in (2, 3):
            if by in (2, PIPES[pipe][3]):
                first_copy(pipe, 0 if by == 2 else 1, 0).start()

    compute_terms(2)
    compute_terms(1)
    forward(1, 2)
    forward(3, 1)
    attend(0)
    compute_terms(3)
    compute_terms(0)
    forward(1, 3)
    forward(3, 0)

    def grad_copy(by):
        return remote(
            grad_out.at[by], grad_in.at[by], core_send.at[2, by], core_recv.at[2, by], partner
        )

    def attn_grad(by):
        for chunk in range(4):
            w_along_x(by, chunk).wait_recv()
        rows = pl.ds(pl.multiple_of(flip(y, by) * HALF, HALF), HALF)

        def one_side(side, carry):
            owner = lax.rem(1 - core + side, 2)
            half = contract(og_pair[owner], weight[rows, :], 1, 1).astype(BF16)

            @pl.when(side == 0)
            def _():
                grad_out[by] = half

            @pl.when(side == 1)
            def _():
                grad_half[by] = half

            return carry

        one_side(0, 0)
        grad_copy(by).start()
        one_side(1, 0)

    def store_copy(by, which):
        cols = pl.ds(pl.multiple_of(flip(y, by) * GROUP, GROUP), GROUP)
        src = (qv, kv, vv)[which]
        dst = (dq_hbm, dk_hbm, dv_hbm)[which]
        return pltpu.make_async_copy(src.at[:, cols], dst.at[:, cols], store_sem.at[which, by])

    def attend_back(by):
        grad_copy(by).wait_recv()
        for t in range(2):
            mine = grad_half[by, :, t * SHARD : (t + 1) * SHARD]
            other = grad_in[by, :, t * SHARD : (t + 1) * SHARD]
            first, second = split_cores(mine, other)
            heads6[:, t * HALF : t * HALF + SHARD] = first
            heads6[:, t * HALF + SHARD : (t + 1) * HALF] = second

        def some_heads(i, carry):
            at = [i * TOGETHER + t for t in range(TOGETHER)]
            heads = [flip(y, by) * 6 + n for n in at]
            cols = [head_cols(head) for head in heads]
            loaded = [
                (qv[:, c], kv[:, c], vv[:, c], probs[head], heads6[:, head_cols(n)])
                for c, head, n in zip(cols, heads, at)
            ]
            products = [contract(g, v, 1, 1) * w.astype(F32) for _, _, v, w, g in loaded]
            totals = [jnp.sum(product, axis=1, keepdims=True) for product in products]
            score_grads = [
                ((product - entry[3].astype(F32) * total) * SCALE).astype(BF16)
                for product, total, entry in zip(products, totals, loaded)
            ]
            grads = [
                (
                    contract(ds, k, 1, 0).astype(BF16),
                    contract(ds, q, 0, 0).astype(BF16),
                    contract(w, g, 0, 0).astype(BF16),
                )
                for ds, (q, k, _, w, g) in zip(score_grads, loaded)
            ]
            for c, (dq, dk, dv) in zip(cols, grads):
                qv[:, c] = dq
                kv[:, c] = dk
                vv[:, c] = dv
            return carry

        lax.fori_loop(0, 6 // TOGETHER, some_heads, 0)
        for which in range(3):
            store_copy(by, which).start()

    def summed(own, others):
        total = own.astype(F32)
        for other in others:
            total += other.astype(F32)
        return total.astype(BF16)

    def second_copy(pipe, part):
        _, _, axes, near = PIPES[pipe]
        far = flip(here_on[axes[0]], 4 - near)
        if pipe == 0:
            place = (flip(y, part),)
        elif pipe == 1:
            place = (slice(None), flip(y, part))
        else:
            place = (pl.ds(part * 2, 2),)
        return remote(
            terms[pipe].at[(far,) + place],
            quads[pipe].at[place],
            rs_send.at[pipe, 8 + part],
            rs_recv.at[pipe, 8 + part],
            along[axes[0]](4 - near),
        )

    def add_to(pipe, first, part, others):
        term = terms[pipe]

        def one_block(i, carry):
            if pipe == 0:
                place = (flip(y, part), i)
            elif pipe == 1:
                place = (i, flip(y, part))
            else:
                place = (part * 2 + lax.div(i, 4), lax.rem(i, 4))
            term[(first,) + place] = summed(
                term[(first,) + place], [other[before + place] for other, before in others]
            )
            return carry

        lax.fori_loop(0, 4 if pipe < 2 else 8, one_block, 0)

    def pipe_second(pipe, parts):
        _, _, axes, near = PIPES[pipe]
        far = flip(here_on[axes[0]], 4 - near)
        for part in parts:
            if pipe < 2 or part == 0:
                first_copy(pipe, 0, part).wait_recv()
            add_to(pipe, far, part, [(pairs[pipe], (0,))])
            second_copy(pipe, part).start()

    def third_copy(pipe, by):
        axes = PIPES[pipe][2]
        return remote(
            terms[pipe].at[here_on[axes[0]], flip(here_on[axes[1]], by)],
            nexts[pipe].at[by - 1],
            rs_send.at[pipe, 11 + by],
            rs_recv.at[pipe, 11 + by],
            along[axes[1]](by),
        )

    def pipe_third(pipe):
        own = here_on[PIPES[pipe][2][0]]
        for part in (2, 1, 3, 0) if pipe < 2 else (0, 1):
            if pipe < 2 or part == 0:
                first_copy(pipe, 1, part).wait_recv()
            second_copy(pipe, part).wait_recv()
            add_to(pipe, own, part, [(pairs[pipe], (1,)), (quads[pipe], ())])
            if pipe == 0 and part > 0:
                third_copy(pipe, part).start()
        if pipe > 0:
            for by in (2, 1, 3):
                third_copy(pipe, by).start()

    def fourth_copy(pipe, by):
        axes = PIPES[pipe][2]
        return remote(
            terms[pipe].at[here_on[axes[0]], here_on[axes[1]], flip(here_on[axes[2]], by)],
            lasts[pipe].at[by - 1],
            rs_send.at[pipe, 14 + by],
            rs_recv.at[pipe, 14 + by],
            along[axes[2]](by),
        )

    def pipe_fourth(pipe):
        term, arrived = terms[pipe], nexts[pipe]
        axes = PIPES[pipe][2]
        own = here_on[axes[0]], here_on[axes[1]]
        for by in (1, 2, 3):
            third_copy(pipe, by).wait_recv()

        def one_block(third, carry):
            place = own + (third,)
            term[place] = summed(term[place], [arrived[r, third] for r in range(3)])
            return carry

        lax.fori_loop(0, 4, one_block, 0)
        for by in (2, 1, 3):
            fourth_copy(pipe, by).start()

    def pipe_last(pipe):
        first_row, count, axes, _ = PIPES[pipe]
        for by in (1, 2, 3):
            fourth_copy(pipe, by).wait_recv()
        dw_rows[first_row : first_row + count, :] = summed(
            terms[pipe][tuple(here_on[axis] for axis in axes)], [lasts[pipe][r] for r in range(3)]
        )

    attn_grad(0)
    attend_back(0)
    forward(2, 0)
    forward(2, 3)
    pipe_second(0, (2, 1))
    pipe_second(1, (2, 1))
    attn_grad(1)
    attend_back(1)
    forward(2, 1)
    forward(2, 2)
    pipe_second(0, (3, 0))
    pipe_second(1, (3, 0))
    attn_grad(3)
    attend_back(3)
    pipe_second(2, (0, 1))
    pipe_second(3, (0, 1))
    attn_grad(2)
    def part_copy(block):
        return remote(
            part_out.at[block], part_in.at[block], core_send.at[3, block], core_recv.at[3, block],
            partner,
        )

    def one_block(block, carry):
        cols = pl.ds(pl.multiple_of(block * WIDE, WIDE), WIDE)
        attn = jnp.concatenate(
            [attn_half[:, group].reshape(2 * ROWS, HALF) for group in range(4)], axis=1
        )
        part[...] = contract(attn, weight[:, cols], 1, 0).reshape(2, ROWS, WIDE)
        part_out[block] = part[1 - core].astype(BF16)
        part_copy(block).start()
        pool[:ROWS, cols] = part[core].astype(BF16)
        return carry

    lax.fori_loop(0, D // WIDE, one_block, 0)

    def add_block(block, carry):
        cols = pl.ds(pl.multiple_of(block * WIDE, WIDE), WIDE)
        part_copy(block).wait_recv()
        pool[:ROWS, cols] = (
            pool[:ROWS, cols].astype(F32) + part_in[block].astype(F32)
        ).astype(BF16)
        return carry

    lax.fori_loop(0, D // WIDE, add_block, 0)

    for by in range(1, 8):
        slots(by, og_slots, 0).wait_send()
    pick(3, 8 * SLOT, ROWS, slot_out)
    for by in range(1, 8):
        slots(by, proj_slots, 1).start()

    for pipe in (0, 1, 2, 3):
        pipe_third(pipe)
    attend_back(2)
    for pipe in (0, 1, 2, 3):
        pipe_fourth(pipe)

    for by in range(1, 8):
        slots(by, proj_slots, 1).wait_recv()
    pool[ROWS:, :] = proj_slots[...]
    og_copy.wait_send()
    pick(1, ROWS, ROWS + 8 * SLOT, og_pair, core)
    proj_copy = pltpu.make_async_copy(og_pair.at[core], proj_hbm, load_sem.at[0])
    proj_copy.start()

    for pipe in (2, 3, 0, 1):
        pipe_last(pipe)
    dw_copy = pltpu.make_async_copy(dw_rows, dw_hbm, load_sem.at[1])
    dw_copy.start()

    for by in range(4):
        for chunk in range(4):
            if by > 0:
                w_along_y(by, chunk).wait_send()
            w_along_x(by, chunk).wait_send()
        attn_copy(by).wait_send()
        grad_copy(by).wait_send()
    for by in range(1, 8):
        slots(by, proj_slots, 1).wait_send()
    for block in range(D // WIDE):
        part_copy(block).wait_send()
    for pipe in range(4):
        for part in range(4) if pipe < 2 else (0,):
            first_copy(pipe, 0, part).wait_send()
            first_copy(pipe, 1, part).wait_send()
        for part in range(4) if pipe < 2 else (0, 1):
            second_copy(pipe, part).wait_send()
        for by in (1, 2, 3):
            third_copy(pipe, by).wait_send()
            fourth_copy(pipe, by).wait_send()
    for by in range(4):
        for which in range(3):
            store_copy(by, which).wait()
    proj_copy.wait()
    dw_copy.wait()


def store_kernel(*refs):
    count = len(refs) // 3
    sources, targets, buffers = refs[:count], refs[count : 2 * count], refs[2 * count : 3 * count]
    load_sem, store_sem = refs[-2:]
    loads, stores = [], []
    for i, (src, dst, held) in enumerate(zip(sources, targets, buffers)):
        rows = src.shape[0] // 3
        for part in range(3):
            at = pl.ds(part * rows, rows)
            loads.append(pltpu.make_async_copy(src.at[at], held.at[at], load_sem.at[i, part]))
            stores.append(pltpu.make_async_copy(held.at[at], dst.at[at], store_sem.at[i, part]))
    for copy in loads:
        copy.start()
    for arrived, copy in zip(loads, stores):
        arrived.wait()
        copy.start()
    for copy in stores:
        copy.wait()


def store(results):
    any_space = pl.BlockSpec(memory_space=pl.ANY)
    return pl.pallas_call(
        store_kernel,
        out_shape=[jax.ShapeDtypeStruct(result.shape, result.dtype) for result in results],
        in_specs=[any_space] * len(results),
        out_specs=[any_space] * len(results),
        scratch_shapes=[pltpu.VMEM(result.shape, result.dtype) for result in results]
        + [pltpu.SemaphoreType.DMA((len(results), 3))] * 2,
        compiler_params=pltpu.CompilerParams(vmem_limit_bytes=63 * 2**20),
        name="store_results",
    )(*results)


def shards(
    queries, key_vectors, value_vectors, image_lengths, image_dest, image_offset, out_weight, out_grad
):
    any_space = pl.BlockSpec(memory_space=pl.ANY)
    rows = jax.ShapeDtypeStruct((ROWS, D), BF16)
    vmem = pltpu.VMEM
    dma = pltpu.SemaphoreType.DMA
    results = pl.pallas_call(
        kernel,
        out_shape=(rows, rows, rows, rows, jax.ShapeDtypeStruct((SHARD, BLOCK), BF16)),
        in_specs=[pl.BlockSpec(memory_space=vmem)] + [any_space] * 5,
        out_specs=[any_space] * 5,
        scratch_shapes=[
            vmem((ROWS, D), BF16),
            vmem((ROWS, D), BF16),
            vmem((ROWS, D), BF16),
            vmem((8 * SHARD, D), BF16),
            vmem((ROWS + 8 * SLOT, D), BF16),
            vmem((8 * SLOT, D), BF16),
            vmem((8 * SLOT, D), BF16),
            vmem((2, ROWS, D), BF16),
            vmem((2, 4, ROWS, HALF), BF16),
            vmem((4, ROWS, HALF), BF16),
            vmem((HALF, 2 * ROWS), BF16),
            vmem((24, ROWS, ROWS), BF16),
            vmem((ROWS, ROWS), F32),
            vmem((ROWS, GROUP), BF16),
            vmem((4, ROWS, HALF), BF16),
            vmem((4, ROWS, HALF), BF16),
            vmem((4, ROWS, HALF), BF16),
            vmem((2, ROWS, WIDE), F32),
            vmem((D // WIDE, ROWS, WIDE), BF16),
            vmem((D // WIDE, ROWS, WIDE), BF16),
            vmem((8 * SLOT, D), BF16),
            *[vmem((4, 4, 4, count, BLOCK), BF16) for _, count, _, _ in PIPES],
            *[vmem((2, 4, 4, count, BLOCK), BF16) for _, count, _, _ in PIPES],
            *[vmem((4, 4, count, BLOCK), BF16) for _, count, _, _ in PIPES],
            *[vmem((3, 4, count, BLOCK), BF16) for _, count, _, _ in PIPES],
            *[vmem((3, count, BLOCK), BF16) for _, count, _, _ in PIPES],
            vmem((SHARD, BLOCK), BF16),
            vmem((ROWS, HD), jnp.int32),
            dma((5,)),
            dma((3, 4)),
            dma((3, 4)),
            dma((3, 4)),
            dma((4, 4)),
            dma((4, 4)),
            dma((2, 7)),
            dma((2, 7)),
            dma((4, 8)),
            dma((4, 8)),
            dma((4, 18)),
            dma((4, 18)),
        ],
        compiler_params=pltpu.CompilerParams(
            collective_id=0, has_side_effects=True, vmem_limit_bytes=63 * 2**20
        ),
        name="attention_step",
    )(
        jnp.concatenate([image_lengths, image_dest, image_offset], axis=1),
        queries,
        key_vectors,
        value_vectors,
        out_weight,
        out_grad,
    )
    return tuple(store(results))


def solution(mesh):
    rows = P(("dp", "fsdp"), None)
    return jax.shard_map(
        shards,
        mesh=mesh,
        in_specs=(rows, rows, rows, P(), P(), P(), P("fsdp", None), rows),
        out_specs=(rows, rows, rows, rows, P("fsdp", "dp")),
        check_vma=False,
    )
```

```python
import jax
import jax.numpy as jnp
from jax import lax
from jax.experimental import pallas as pl
from jax.experimental.pallas import tpu as pltpu
from jax.sharding import PartitionSpec as P

HD = 128
SLOT = 16
MESH = pl.DeviceIdType.MESH
F32 = jnp.float32
BF16 = jnp.bfloat16
ROWS = 288
D = 3072
GROUP = 768
HALF = 384
SHARD = 192
CHUNK = 48
RELAYED = ((1, 0), (3, 3))
BLOCK = 384
PIPES = ((0, 64, "zyx", 1), (64, 48, "zxy", 3), (112, 48, "yzx", 1), (160, 32, "yxz", 3))
SCALE = HD ** (-0.5)
LOG2_E = 1.4426950408889634
TOGETHER = 2
WIDE = 512


def flip(index, by):
    high = lax.rem(lax.div(index, 2) + by // 2, 2)
    return high * 2 + lax.rem(lax.rem(index, 2) + by % 2, 2)


def contract(first, second, first_dim, second_dim):
    return lax.dot_general(
        first, second, (((first_dim,), (second_dim,)), ((), ())), preferred_element_type=F32
    )


def kernel(
    images,
    q_hbm,
    k_hbm,
    v_hbm,
    w_hbm,
    og_hbm,
    proj_hbm,
    dq_hbm,
    dk_hbm,
    dv_hbm,
    dw_hbm,
    qv,
    kv,
    vv,
    weight,
    pool,
    og_slots,
    slot_out,
    og_pair,
    attn_half,
    attn_out,
    attn_t,
    probs,
    bias,
    heads6,
    grad_both,
    grad_half,
    grad_out,
    grad_in,
    part,
    part_out,
    part_in,
    proj_slots,
    term_0,
    term_1,
    term_2,
    term_3,
    pair_0,
    pair_1,
    pair_2,
    pair_3,
    quad_0,
    quad_1,
    quad_2,
    quad_3,
    next_0,
    next_1,
    next_2,
    next_3,
    last_0,
    last_1,
    last_2,
    last_3,
    dw_rows,
    table,
    load_sem,
    store_sem,
    wy_send,
    wy_recv,
    wx_send,
    wx_recv,
    a2a_send,
    a2a_recv,
    core_send,
    core_recv,
    rs_send,
    rs_recv,
):
    dp = lax.axis_index("dp")
    fs = lax.axis_index("fsdp")
    xh, z = lax.div(dp, 4), lax.rem(dp, 4)
    y, xl, core = lax.div(fs, 4), lax.rem(lax.div(fs, 2), 2), lax.rem(fs, 2)

    def device(xh_, xl_, y_, z_, core_):
        return (xh_ * 4 + z_, y_ * 4 + xl_ * 2 + core_)

    def along_x(by):
        return device(lax.rem(xh + by // 2, 2), lax.rem(xl + by % 2, 2), y, z, core)

    def along_y(by):
        return device(xh, xl, flip(y, by), z, core)

    def along_z(by):
        return device(xh, xl, y, flip(z, by), core)

    def over_dp(by):
        return device(lax.rem(xh + by // 4, 2), xl, y, flip(z, by % 4), core)

    partner = device(xh, xl, y, z, 1 - core)

    def remote(src, dst, send, recv, target):
        return pltpu.make_async_remote_copy(
            src_ref=src, dst_ref=dst, send_sem=send, recv_sem=recv, device_id=target, device_id_type=MESH
        )

    here = y * 2 + xl
    loads = [
        pltpu.make_async_copy(
            w_hbm, weight.at[pl.ds(pl.multiple_of(here * SHARD, SHARD), SHARD)], load_sem.at[0, 0]
        ),
        pltpu.make_async_copy(og_hbm, pool.at[0:ROWS], load_sem.at[1, 0]),
    ]

    def head_load(which, by):
        cols = pl.ds(pl.multiple_of(flip(y, by) * GROUP, GROUP), GROUP)
        src, dst = (q_hbm, k_hbm, v_hbm)[which], (qv, kv, vv)[which]
        return pltpu.make_async_copy(src.at[:, cols], dst.at[:, cols], load_sem.at[2 + which, by])

    for which in range(3):
        head_load(which, 2).start()
    for copy in loads:
        copy.start()
    for by in (1, 3, 0):
        for which in range(3):
            head_load(which, by).start()
    barrier = pltpu.get_barrier_semaphore()
    peers = (
        [along_x(by) for by in (1, 2, 3)]
        + [along_y(by) for by in (1, 2, 3)]
        + [along_z(by) for by in (1, 2, 3)]
        + [over_dp(by) for by in (5, 6, 7)]
        + [partner]
    )
    for peer in peers:
        pl.semaphore_signal(barrier, inc=1, device_id=peer, device_id_type=MESH)

    width = images.shape[1] // 3

    def images_of(dp_):
        rows = pl.ds(dp_ * 16 + fs, 1)
        length, dest, offset = (images[rows, i * width : (i + 1) * width] for i in range(3))
        lane = lax.broadcasted_iota(jnp.int32, length.shape, 1)
        start = jnp.zeros_like(length)
        for image in range(length.shape[1] - 1):
            start += jnp.where(lane > image, length[:, image : image + 1], 0)
        return length, dest, offset, start

    def sum_lanes(hit, value):
        return jnp.sum(jnp.where(hit, value, 0), axis=1, keepdims=True)

    row = lax.broadcasted_iota(jnp.int32, (ROWS, 1), 0)
    own_length, own_dest, own_offset, own_start = images_of(dp)
    columns = lax.broadcasted_iota(jnp.int32, (1, ROWS), 1)
    row_image = jnp.zeros((ROWS, 1), jnp.int32)
    column_image = jnp.zeros((1, ROWS), jnp.int32)
    for image in range(1, width):
        first = own_start[:, image : image + 1]
        row_image += jnp.where(row >= first, 1, 0)
        column_image += jnp.where(columns >= first, 1, 0)
    bias[...] = jnp.where(row_image == column_image, 0.0, -1e30).astype(F32)

    def head_cols(head):
        return pl.ds(pl.multiple_of(head * HD, HD), HD)

    def split_cores(first, second):
        mine = jnp.where(core == 0, first, second)
        other = jnp.where(core == 0, second, first)
        return mine, other

    def attend_heads(by):
        group = flip(y, by)
        for which in range(3):
            head_load(which, by).wait()

        def some_heads(i, carry):
            at = [i * TOGETHER + t for t in range(TOGETHER)]
            cols = [head_cols(group * 6 + n) for n in at]
            loaded = [(qv[:, c], kv[:, c], vv[:, c]) for c in cols]
            scores = [contract(q, k, 1, 1) * (SCALE * LOG2_E) + bias[...] for q, k, _ in loaded]
            powers = [jnp.exp2(score - jnp.max(score, axis=1, keepdims=True)) for score in scores]
            weights = [
                (power * (1.0 / jnp.sum(power, axis=1, keepdims=True))).astype(BF16)
                for power in powers
            ]
            mixed = [contract(w, v, 1, 0).astype(BF16) for w, (_, _, v) in zip(weights, loaded)]
            for n, w, attn in zip(at, weights, mixed):
                probs[group * 6 + n] = w
                heads6[:, head_cols(n)] = attn
            return carry

        lax.fori_loop(0, 6 // TOGETHER, some_heads, 0)

    attend_heads(2)
    senders = [images_of(sender) for sender in range(8)]
    first_rows = lax.broadcasted_iota(jnp.int32, (SLOT, 1), 0) + 1
    for sender, (_, dest, offset, _) in enumerate(senders):
        arrives = (dest == dp) & (dp != sender)
        table[sender * SLOT : (sender + 1) * SLOT, 2:3] = (
            sum_lanes(arrives, offset + first_rows) - 1
        )

    pl.semaphore_wait(barrier, len(peers))

    def shard_rows(y_, xl_, chunk):
        return pl.ds(pl.multiple_of((y_ * 2 + xl_) * SHARD + chunk * CHUNK, CHUNK), CHUNK)

    def w_along_y(by, chunk):
        via = (1 if chunk < 2 else 3) if by == 2 else 0
        rows = weight.at[shard_rows(flip(y, via), xl, chunk)]
        return remote(
            rows,
            rows,
            wy_send.at[by - 1, chunk],
            wy_recv.at[by - 1, chunk],
            along_y(4 - via if by == 2 else by),
        )

    def w_along_x(by, chunk):
        if (by, chunk) in RELAYED:
            rows = weight.at[shard_rows(y, 1 - xl, chunk)]
            return remote(
                rows, rows, wx_send.at[by, chunk], wx_recv.at[by, chunk], along_y(by)
            )
        rows = weight.at[shard_rows(flip(y, by), xl, chunk)]
        return remote(
            rows,
            rows,
            wx_send.at[by, chunk],
            wx_recv.at[by, chunk],
            along_x(1 if chunk % 2 == 0 else 3),
        )

    def forward(by, chunk):
        w_along_y(by, chunk).wait_recv()
        if by == (1 if chunk < 2 else 3):
            w_along_y(2, chunk).start()
        if (by, chunk) not in RELAYED:
            w_along_x(by, chunk).start()

    def relay(by, chunk):
        w_along_x(0, chunk).wait_recv()
        w_along_x(by, chunk).start()

    loads[0].wait()
    for step in range(4):
        w_along_y(1, step).start()
        w_along_y(3, 3 - step).start()
    w_along_x(0, 0).start()
    w_along_x(0, 3).start()

    def pick(column, out_rows, in_rows, dst, dst_core=None, then=None):
        chosen = lax.broadcasted_iota(jnp.int32, (out_rows, in_rows), 1) == (
            table[:out_rows, column : column + 1]
        )
        one_hot = jnp.where(chosen, 1.0, 0.0).astype(BF16)

        def one_part(i, carry):
            cols = pl.ds(pl.multiple_of(i * GROUP, GROUP), GROUP)
            rows = contract(one_hot, pool[:in_rows, cols], 1, 0).astype(BF16)
            if dst_core is None:
                dst[:, cols] = rows
            else:
                dst[dst_core, :, cols] = rows
            if then is not None:
                then(i).start()
            return carry

        lax.fori_loop(0, D // GROUP, one_part, 0)

    def unit(index):
        return pl.ds(pl.multiple_of(index * SLOT, SLOT), SLOT)

    def slots(by, dst, phase):
        to_dp = lax.rem(xh + by // 4, 2) * 4 + flip(z, by % 4)
        return remote(
            slot_out.at[unit(to_dp)],
            dst.at[unit(dp)],
            a2a_send.at[phase, by - 1],
            a2a_recv.at[phase, by - 1],
            over_dp(by),
        )

    loads[1].wait()
    pick(2, 8 * SLOT, ROWS, slot_out)
    own_slot = jnp.zeros((SLOT, D), BF16)
    og_slots[unit(dp), :] = own_slot
    proj_slots[unit(dp), :] = own_slot
    for by in range(1, 8):
        slots(by, og_slots, 0).start()
    w_along_x(0, 1).start()
    w_along_x(0, 2).start()
    length, dest, offset, start = [jnp.concatenate(list(part), axis=1) for part in zip(*senders)]
    sender = lax.div(lax.broadcasted_iota(jnp.int32, length.shape, 1), width)
    covers = (dest == dp) & (row >= offset) & (row < offset + length)
    table[:, 1:2] = sum_lanes(
        covers, jnp.where(sender == dp, start, ROWS + SLOT * sender) - offset + row
    )
    slot_row = lax.broadcasted_iota(jnp.int32, (8 * SLOT, 1), 0)
    slot, in_slot = lax.div(slot_row, SLOT), lax.rem(slot_row, SLOT)
    inside = (row >= own_start) & (row < own_start + own_length)
    table[:, 0:1] = sum_lanes(
        inside, jnp.where(own_dest == dp, own_offset, ROWS + SLOT * own_dest) - own_start + row
    )
    table[: 8 * SLOT, 3:4] = (
        sum_lanes((own_dest == slot) & (own_dest != dp), own_start + in_slot + 1) - 1
    )


    def attn_copy(by):
        group = flip(y, by)
        return remote(
            attn_out.at[group],
            attn_half.at[core, group],
            core_send.at[0, by],
            core_recv.at[0, by],
            partner,
        )

    def attend_send(by):
        group = flip(y, by)
        for t in range(2):
            first = heads6[:, t * HALF : t * HALF + SHARD]
            second = heads6[:, t * HALF + SHARD : (t + 1) * HALF]
            mine, other = split_cores(first, second)
            attn_half[core, group, :, t * SHARD : (t + 1) * SHARD] = mine
            attn_out[group, :, t * SHARD : (t + 1) * SHARD] = other
        attn_copy(by).start()

    def attend(by):
        attend_heads(by)
        attend_send(by)

    attend_send(2)
    attend(1)
    for by, chunk in RELAYED:
        relay(by, chunk)
    forward(1, 0)
    forward(3, 3)

    for by in range(1, 8):
        slots(by, og_slots, 0).wait_recv()
    pool[ROWS:, :] = og_slots[...]
    pick(0, ROWS, ROWS + 8 * SLOT, og_pair, core)
    og_copy = remote(
        og_pair.at[core], og_pair.at[core], core_send.at[1, 0], core_recv.at[1, 0], partner
    )
    og_copy.start()
    attend(3)
    forward(1, 1)
    forward(3, 2)
    og_copy.wait_recv()

    grad_scale = (ROWS * 128) ** (-0.5)

    x = xh * 2 + xl
    here_on = {"x": x, "y": y, "z": z}
    along = {"x": along_x, "y": along_y, "z": along_z}
    terms = (term_0, term_1, term_2, term_3)
    pairs = (pair_0, pair_1, pair_2, pair_3)
    quads = (quad_0, quad_1, quad_2, quad_3)
    nexts = (next_0, next_1, next_2, next_3)
    lasts = (last_0, last_1, last_2, last_3)

    def first_copy(pipe, slot, by):
        _, _, axes, near = PIPES[pipe]
        toward = flip(here_on[axes[0]], 2 if slot == 0 else near)
        term, pair, group = terms[pipe], pairs[pipe], flip(y, by)
        if pipe == 0:
            src, dst = term.at[toward, group], pair.at[slot, group]
        elif pipe == 1:
            src, dst = term.at[toward, :, group], pair.at[slot, :, group]
        else:
            src, dst = term.at[toward], pair.at[slot]
        sem = slot * 4 + by
        return remote(src, dst, rs_send.at[pipe, sem], rs_recv.at[pipe, sem], along[axes[0]](near))

    def compute_terms(by):
        group = flip(y, by)
        attn_copy(by).wait_recv()
        attn_t[...] = attn_half[:, group].reshape(2 * ROWS, HALF).T
        for by_z in (2, 1, 3, 0):
            z_ = flip(z, by_z)

            columns_of = [
                pl.ds(pl.multiple_of((xh_ * 4 + z_) * BLOCK, BLOCK), BLOCK) for xh_ in range(2)
            ]
            grads = jnp.concatenate(
                [og_pair[:, :, cols].reshape(2 * ROWS, BLOCK) for cols in columns_of], axis=1
            )
            term = (contract(attn_t[...], grads, 1, 0) * grad_scale).astype(BF16)
            for x_ in range(4):
                places = ((z_, group, x_), (z_, x_, group), (group, z_, x_), (group, x_, z_))
                left = (x_ // 2) * BLOCK
                for (first_row, count, _, _), buffer, place in zip(PIPES, terms, places):
                    at = (x_ % 2) * SHARD + first_row
                    buffer[place] = term[at : at + count, left : left + BLOCK]
            for pipe in range(2):
                if by_z in (2, PIPES[pipe][3]):
                    first_copy(pipe, 0 if by_z == 2 else 1, by).start()
        for pipe in (2, 3):
            if by in (2, PIPES[pipe][3]):
                first_copy(pipe, 0 if by == 2 else 1, 0).start()

    compute_terms(2)
    compute_terms(1)
    forward(1, 2)
    forward(3, 1)
    attend(0)
    compute_terms(3)
    compute_terms(0)
    forward(1, 3)
    forward(3, 0)

    def grad_copy(by):
        return remote(
            grad_out.at[by], grad_in.at[by], core_send.at[2, by], core_recv.at[2, by], partner
        )

    def attn_grad(by):
        for chunk in range(4):
            if by > 0 or chunk not in [relayed for _, relayed in RELAYED]:
                w_along_x(by, chunk).wait_recv()
        rows = pl.ds(pl.multiple_of(flip(y, by) * HALF, HALF), HALF)

        both = contract(og_pair[...].reshape(2 * ROWS, D), weight[rows, :], 1, 1)
        grad_both[...] = both.astype(BF16).reshape(2, ROWS, HALF)
        grad_out[by] = grad_both[1 - core]
        grad_copy(by).start()
        grad_half[by] = grad_both[core]

    def store_copy(by, which):
        cols = pl.ds(pl.multiple_of(flip(y, by) * GROUP, GROUP), GROUP)
        src = (qv, kv, vv)[which]
        dst = (dq_hbm, dk_hbm, dv_hbm)[which]
        return pltpu.make_async_copy(src.at[:, cols], dst.at[:, cols], store_sem.at[which, by])

    def attend_back(by):
        grad_copy(by).wait_recv()
        for t in range(2):
            mine = grad_half[by, :, t * SHARD : (t + 1) * SHARD]
            other = grad_in[by, :, t * SHARD : (t + 1) * SHARD]
            first, second = split_cores(mine, other)
            heads6[:, t * HALF : t * HALF + SHARD] = first
            heads6[:, t * HALF + SHARD : (t + 1) * HALF] = second

        def some_heads(i, carry):
            at = [i * TOGETHER + t for t in range(TOGETHER)]
            heads = [flip(y, by) * 6 + n for n in at]
            cols = [head_cols(head) for head in heads]
            loaded = [
                (qv[:, c], kv[:, c], vv[:, c], probs[head], heads6[:, head_cols(n)])
                for c, head, n in zip(cols, heads, at)
            ]
            products = [contract(g, v, 1, 1) * w.astype(F32) for _, _, v, w, g in loaded]
            totals = [jnp.sum(product, axis=1, keepdims=True) for product in products]
            score_grads = [
                (product - entry[3].astype(F32) * total).astype(BF16)
                for product, total, entry in zip(products, totals, loaded)
            ]
            grads = [
                (
                    (contract(ds, k, 1, 0) * SCALE).astype(BF16),
                    (contract(ds, q, 0, 0) * SCALE).astype(BF16),
                    contract(w, g, 0, 0).astype(BF16),
                )
                for ds, (q, k, _, w, g) in zip(score_grads, loaded)
            ]
            for c, (dq, dk, dv) in zip(cols, grads):
                qv[:, c] = dq
                kv[:, c] = dk
                vv[:, c] = dv
            return carry

        lax.fori_loop(0, 6 // TOGETHER, some_heads, 0)
        for which in range(3):
            store_copy(by, which).start()

    def summed(own, others):
        total = own.astype(F32)
        for other in others:
            total += other.astype(F32)
        return total.astype(BF16)

    def second_copy(pipe, part):
        _, _, axes, near = PIPES[pipe]
        far = flip(here_on[axes[0]], 4 - near)
        if pipe == 0:
            place = (flip(y, part),)
        elif pipe == 1:
            place = (slice(None), flip(y, part))
        else:
            place = (pl.ds(part * 2, 2),)
        return remote(
            terms[pipe].at[(far,) + place],
            quads[pipe].at[place],
            rs_send.at[pipe, 8 + part],
            rs_recv.at[pipe, 8 + part],
            along[axes[0]](4 - near),
        )

    def add_to(pipe, first, part, others):
        term = terms[pipe]

        def one_block(i, carry):
            if pipe == 0:
                place = (flip(y, part), i)
            elif pipe == 1:
                place = (i, flip(y, part))
            else:
                place = (part * 2 + lax.div(i, 4), lax.rem(i, 4))
            term[(first,) + place] = summed(
                term[(first,) + place], [other[before + place] for other, before in others]
            )
            return carry

        lax.fori_loop(0, 4 if pipe < 2 else 8, one_block, 0)

    def pipe_second(pipe, parts):
        _, _, axes, near = PIPES[pipe]
        far = flip(here_on[axes[0]], 4 - near)
        for part in parts:
            if pipe < 2 or part == 0:
                first_copy(pipe, 0, part).wait_recv()
            add_to(pipe, far, part, [(pairs[pipe], (0,))])
            second_copy(pipe, part).start()

    def third_copy(pipe, by):
        axes = PIPES[pipe][2]
        return remote(
            terms[pipe].at[here_on[axes[0]], flip(here_on[axes[1]], by)],
            nexts[pipe].at[by - 1],
            rs_send.at[pipe, 11 + by],
            rs_recv.at[pipe, 11 + by],
            along[axes[1]](by),
        )

    def pipe_third(pipe):
        own = here_on[PIPES[pipe][2][0]]
        for part in (2, 1, 3, 0) if pipe < 2 else (0, 1):
            if pipe < 2 or part == 0:
                first_copy(pipe, 1, part).wait_recv()
            second_copy(pipe, part).wait_recv()
            add_to(pipe, own, part, [(pairs[pipe], (1,)), (quads[pipe], ())])
            if pipe == 0 and part > 0:
                third_copy(pipe, part).start()
        if pipe > 0:
            for by in (2, 1, 3):
                third_copy(pipe, by).start()

    def fourth_copy(pipe, by):
        axes = PIPES[pipe][2]
        return remote(
            terms[pipe].at[here_on[axes[0]], here_on[axes[1]], flip(here_on[axes[2]], by)],
            lasts[pipe].at[by - 1],
            rs_send.at[pipe, 14 + by],
            rs_recv.at[pipe, 14 + by],
            along[axes[2]](by),
        )

    def pipe_fourth(pipe):
        term, arrived = terms[pipe], nexts[pipe]
        axes = PIPES[pipe][2]
        own = here_on[axes[0]], here_on[axes[1]]
        for by in (1, 2, 3):
            third_copy(pipe, by).wait_recv()

        def one_block(third, carry):
            place = own + (third,)
            term[place] = summed(term[place], [arrived[r, third] for r in range(3)])
            return carry

        lax.fori_loop(0, 4, one_block, 0)
        for by in (2, 1, 3):
            fourth_copy(pipe, by).start()

    def pipe_last(pipe):
        first_row, count, axes, _ = PIPES[pipe]
        for by in (1, 2, 3):
            fourth_copy(pipe, by).wait_recv()
        dw_rows[first_row : first_row + count, :] = summed(
            terms[pipe][tuple(here_on[axis] for axis in axes)], [lasts[pipe][r] for r in range(3)]
        )

    attn_grad(0)
    forward(2, 0)
    forward(2, 3)
    pipe_second(0, (2, 1))
    pipe_second(1, (2, 1))
    attend_back(0)
    attn_grad(1)
    forward(2, 1)
    forward(2, 2)
    attend_back(1)
    pipe_second(0, (3, 0))
    pipe_second(1, (3, 0))
    attn_grad(3)
    pipe_second(2, (0, 1))
    pipe_second(3, (0, 1))
    attn_grad(2)
    def part_copy(block):
        return remote(
            part_out.at[block], part_in.at[block], core_send.at[3, block], core_recv.at[3, block],
            partner,
        )

    def one_block(block, carry):
        cols = pl.ds(pl.multiple_of(block * WIDE, WIDE), WIDE)
        attn = jnp.concatenate(
            [attn_half[:, group].reshape(2 * ROWS, HALF) for group in range(4)], axis=1
        )
        part[...] = contract(attn, weight[:, cols], 1, 0).reshape(2, ROWS, WIDE)
        part_out[block] = part[1 - core].astype(BF16)
        part_copy(block).start()
        pool[:ROWS, cols] = part[core].astype(BF16)
        return carry

    lax.fori_loop(0, D // WIDE, one_block, 0)

    def add_block(block, carry):
        cols = pl.ds(pl.multiple_of(block * WIDE, WIDE), WIDE)
        part_copy(block).wait_recv()
        pool[:ROWS, cols] = (
            pool[:ROWS, cols].astype(F32) + part_in[block].astype(F32)
        ).astype(BF16)
        return carry

    lax.fori_loop(0, D // WIDE, add_block, 0)

    for by in range(1, 8):
        slots(by, og_slots, 0).wait_send()
    pick(3, 8 * SLOT, ROWS, slot_out)
    for by in range(1, 8):
        slots(by, proj_slots, 1).start()

    attend_back(3)
    for pipe in (0, 1, 2, 3):
        pipe_third(pipe)
    attend_back(2)
    for pipe in (0, 1, 2, 3):
        pipe_fourth(pipe)

    for by in range(1, 8):
        slots(by, proj_slots, 1).wait_recv()
    pool[ROWS:, :] = proj_slots[...]
    og_copy.wait_send()

    def proj_copy(i):
        cols = pl.ds(pl.multiple_of(i * GROUP, GROUP), GROUP)
        return pltpu.make_async_copy(
            og_pair.at[core, :, cols], proj_hbm.at[:, cols], load_sem.at[0, i]
        )

    pick(1, ROWS, ROWS + 8 * SLOT, og_pair, core, proj_copy)

    for pipe in (2, 3, 0, 1):
        pipe_last(pipe)
    dw_copy = pltpu.make_async_copy(dw_rows, dw_hbm, load_sem.at[1, 0])
    dw_copy.start()

    for by in range(4):
        for chunk in range(4):
            if by > 0:
                w_along_y(by, chunk).wait_send()
            w_along_x(by, chunk).wait_send()
        attn_copy(by).wait_send()
        grad_copy(by).wait_send()
    for by in range(1, 8):
        slots(by, proj_slots, 1).wait_send()
    for block in range(D // WIDE):
        part_copy(block).wait_send()
    for pipe in range(4):
        for part in range(4) if pipe < 2 else (0,):
            first_copy(pipe, 0, part).wait_send()
            first_copy(pipe, 1, part).wait_send()
        for part in range(4) if pipe < 2 else (0, 1):
            second_copy(pipe, part).wait_send()
        for by in (1, 2, 3):
            third_copy(pipe, by).wait_send()
            fourth_copy(pipe, by).wait_send()
    for by in range(4):
        for which in range(3):
            store_copy(by, which).wait()
    for i in range(D // GROUP):
        proj_copy(i).wait()
    dw_copy.wait()


def store_kernel(*refs):
    count = len(refs) // 3
    sources, targets, buffers = refs[:count], refs[count : 2 * count], refs[2 * count : 3 * count]
    load_sem, store_sem = refs[-2:]
    loads, stores = [], []
    for i, (src, dst, held) in enumerate(zip(sources, targets, buffers)):
        rows = src.shape[0] // 3
        for part in range(3):
            at = pl.ds(part * rows, rows)
            loads.append(pltpu.make_async_copy(src.at[at], held.at[at], load_sem.at[i, part]))
            stores.append(pltpu.make_async_copy(held.at[at], dst.at[at], store_sem.at[i, part]))
    for copy in loads:
        copy.start()
    for arrived, copy in zip(loads, stores):
        arrived.wait()
        copy.start()
    for copy in stores:
        copy.wait()


def store(results):
    any_space = pl.BlockSpec(memory_space=pl.ANY)
    return pl.pallas_call(
        store_kernel,
        out_shape=[jax.ShapeDtypeStruct(result.shape, result.dtype) for result in results],
        in_specs=[any_space] * len(results),
        out_specs=[any_space] * len(results),
        scratch_shapes=[pltpu.VMEM(result.shape, result.dtype) for result in results]
        + [pltpu.SemaphoreType.DMA((len(results), 3))] * 2,
        compiler_params=pltpu.CompilerParams(vmem_limit_bytes=63 * 2**20),
        name="store_results",
    )(*results)


def shards(
    queries, key_vectors, value_vectors, image_lengths, image_dest, image_offset, out_weight, out_grad
):
    any_space = pl.BlockSpec(memory_space=pl.ANY)
    rows = jax.ShapeDtypeStruct((ROWS, D), BF16)
    vmem = pltpu.VMEM
    dma = pltpu.SemaphoreType.DMA
    results = pl.pallas_call(
        kernel,
        out_shape=(rows, rows, rows, rows, jax.ShapeDtypeStruct((SHARD, BLOCK), BF16)),
        in_specs=[pl.BlockSpec(memory_space=vmem)] + [any_space] * 5,
        out_specs=[any_space] * 5,
        scratch_shapes=[
            vmem((ROWS, D), BF16),
            vmem((ROWS, D), BF16),
            vmem((ROWS, D), BF16),
            vmem((8 * SHARD, D), BF16),
            vmem((ROWS + 8 * SLOT, D), BF16),
            vmem((8 * SLOT, D), BF16),
            vmem((8 * SLOT, D), BF16),
            vmem((2, ROWS, D), BF16),
            vmem((2, 4, ROWS, HALF), BF16),
            vmem((4, ROWS, HALF), BF16),
            vmem((HALF, 2 * ROWS), BF16),
            vmem((24, ROWS, ROWS), BF16),
            vmem((ROWS, ROWS), F32),
            vmem((ROWS, GROUP), BF16),
            vmem((2, ROWS, HALF), BF16),
            vmem((4, ROWS, HALF), BF16),
            vmem((4, ROWS, HALF), BF16),
            vmem((4, ROWS, HALF), BF16),
            vmem((2, ROWS, WIDE), F32),
            vmem((D // WIDE, ROWS, WIDE), BF16),
            vmem((D // WIDE, ROWS, WIDE), BF16),
            vmem((8 * SLOT, D), BF16),
            *[vmem((4, 4, 4, count, BLOCK), BF16) for _, count, _, _ in PIPES],
            *[vmem((2, 4, 4, count, BLOCK), BF16) for _, count, _, _ in PIPES],
            *[vmem((4, 4, count, BLOCK), BF16) for _, count, _, _ in PIPES],
            *[vmem((3, 4, count, BLOCK), BF16) for _, count, _, _ in PIPES],
            *[vmem((3, count, BLOCK), BF16) for _, count, _, _ in PIPES],
            vmem((SHARD, BLOCK), BF16),
            vmem((ROWS, HD), jnp.int32),
            dma((5, 4)),
            dma((3, 4)),
            dma((3, 4)),
            dma((3, 4)),
            dma((4, 4)),
            dma((4, 4)),
            dma((2, 7)),
            dma((2, 7)),
            dma((4, 8)),
            dma((4, 8)),
            dma((4, 18)),
            dma((4, 18)),
        ],
        compiler_params=pltpu.CompilerParams(
            collective_id=0, has_side_effects=True, vmem_limit_bytes=63 * 2**20
        ),
        name="attention_step",
    )(
        jnp.concatenate([image_lengths, image_dest, image_offset], axis=1),
        queries,
        key_vectors,
        value_vectors,
        out_weight,
        out_grad,
    )
    return tuple(store(results))


def solution(mesh):
    rows = P(("dp", "fsdp"), None)
    return jax.shard_map(
        shards,
        mesh=mesh,
        in_specs=(rows, rows, rows, P(), P(), P(), P("fsdp", None), rows),
        out_specs=(rows, rows, rows, rows, P("fsdp", "dp")),
        check_vma=False,
    )
```
